32 devices in a mesh: parts: 2 (over x), replica: 2 (over core), tensor: 8 (over z, y).
Axes of the slice: x: 2, y: 2, z: 4, core: 2. Of those that a mesh axis runs over, the one named last changes fastest.
Arguments:
- hidden: bfloat16 [256, 8192], P(('parts', 'replica', 'tensor')), parts along dimension 0, may hold values from -6 to 6
- gain: float32 [8192], replicated, may hold values from 0.1 to 1.9
- request_adapter_index: int32 [256], P(('parts', 'replica', 'tensor')), parts along dimension 0, may hold values from 0 to 63
- lengths: int32 [256], P(('parts', 'replica', 'tensor')), parts along dimension 0, may hold values from 1 to 128, as said below
- rotated_key_cache: bfloat16 [256, 1, 128, 128], P(('parts', 'replica', 'tensor')), parts along dimension 0, may hold values from -160 to 160
- earlier_value_cache: bfloat16 [256, 1, 128, 128], P(('parts', 'replica', 'tensor')), parts along dimension 0, may hold values from -6 to 6
- query_weight: bfloat16 [8192, 1024], P(None, 'tensor'), may hold values from -0.0625 to 0.0625
- key_value_weight: bfloat16 [8192, 256], P(None, 'tensor'), may hold values from -0.0625 to 0.0625
- output_weight: bfloat16 [1024, 8192], P('tensor'), may hold values from -0.1875 to 0.1875
- down_weight_qkv: bfloat16 [8192, 64, 192], P('tensor', 'replica'), may hold values from -0.0625 to 0.0625
- up_weight_query: bfloat16 [64, 64, 1024], P(None, 'replica', 'tensor'), may hold values from -0.75 to 0.75
- up_weight_key_value: bfloat16 [64, 64, 256], P(None, 'replica', 'tensor'), may hold values from -0.75 to 0.75
- down_weight_output: bfloat16 [1024, 64, 64], P('tensor', 'replica'), may hold values from -0.1875 to 0.1875
- up_weight_output: bfloat16 [64, 64, 8192], P(None, 'replica', 'tensor'), may hold values from -0.75 to 0.75
Outputs:
- attn_out: bfloat16 [256, 8192], P(('parts', 'replica', 'tensor')), parts along dimension 0
The draws below stay inside these ranges and needn't reach their ends.
There are 2 independent parts, one for each index of `parts`. The reference program is written for one: setup_inputs(seed, part) draws one part's arguments, and reference() takes and returns one part's arrays. A program takes and returns all parts, laid end to end along the dimension named above; an argument that names none is the same for every part. Nothing has to cross between parts.
Inputs may be any that keep to these rules, and one draw needn't show every extreme that they name: `lengths`: some request of every draw has 128 cached positions.
All inputs are finite; a program needn't handle non-finite values.
Results may differ from the reference program's by a relative error of at most 0.015.
The reference program's roundings to bfloat16 on the way count: a program that leaves them out, or rounds other values in their place, can miss the bound.
Values may be sent and summed in bfloat16 or wider, within the bound.
A program may use at most 128 MiB of HBM per device.

```python
import math
import jax
import jax.numpy as jnp
import numpy as np
from jax import lax

MODEL_WIDTH = 8192
HEAD_WIDTH = 128
ADAPTER_RANK = 64
QUERY_HEADS = 8
KEY_VALUE_HEADS = 1
ROWS = 128
ADAPTER_TOTAL = 64
LMAX = 128


def draw_lengths(key, part):
    key = jax.random.fold_in(key, 7)
    values = jax.random.randint(key, (ROWS,), 1, LMAX + 1)
    return values.at[0].set(LMAX).astype(jnp.int32)


def draw_rotated_key_cache(key, part):
    key = jax.random.fold_in(key, 11)
    noise_key = jax.random.fold_in(key, 0)
    noise = jnp.clip(jax.random.normal(noise_key, (ROWS, KEY_VALUE_HEADS, LMAX, HEAD_WIDTH), jnp.float32), -6.0, 6.0)
    values = noise
    return values.astype(jnp.bfloat16)


def place_ends(drawn, key, low, top_value):
    longest = drawn.shape.index(max(drawn.shape))
    spots = []
    for shift in (0, 1):
        where = [jax.random.randint(jax.random.fold_in(key, axis), (), 0, length) for axis, length in enumerate(drawn.shape)]
        where[longest] = (where[longest] + shift) % drawn.shape[longest]
        spots.append(tuple(where))
    return drawn.at[spots[0]].set(low).at[spots[1]].set(top_value)


def block_scale(stream_key, dims, cuts, smallest, largest):
    level, own = 1.0, jax.random.fold_in(stream_key, 6)
    for position, blocks in cuts:
        heights = jnp.exp(jax.random.uniform(jax.random.fold_in(own, position), (blocks,), jnp.float32, smallest / len(cuts), largest / len(cuts)))
        level = level * jnp.repeat(heights, dims[position] // blocks).reshape([-1 if axis == position else 1 for axis in range(len(dims))])
    return level


def cumulative_ranks(amount, lean):
    portions = [(1 << 20) // math.isqrt(standing ** lean) + 1 for standing in range(1, amount + 1)]
    scale = 1 + sum(portions) // (1 << 30)
    return np.cumsum(np.array([max(1, weight // scale) for weight in portions]))


def skewed_ids(rng, shape, count, slope):
    grid = cumulative_ranks(count, slope)
    lot = jax.random.randint(jax.random.fold_in(rng, 1), shape, 0, int(grid[count - 1]))
    rank = jnp.searchsorted(jnp.asarray(grid, jnp.int32), lot, side="right")
    return jax.random.permutation(jax.random.fold_in(rng, 2), count)[rank].astype(jnp.int32)


def centred(rng, extent, width, most, cuts=(), kind=jnp.bfloat16):
    drawn = width * jax.random.normal(rng, extent, jnp.float32)
    if cuts:
        drawn = drawn * block_scale(rng, extent, cuts, -0.22, 0.18)
    return jnp.clip(drawn, -most, most).astype(kind)


def setup_inputs(seed: int = 0, part: int = 0) -> dict:
    key_list = jax.random.split(jax.random.key(seed), 15)
    part_splits = jax.random.split(jax.random.fold_in(key_list[14], part), 15)
    return {
        "hidden": centred(part_splits[0], (ROWS, MODEL_WIDTH), 1.0, 6.0, ((0, 16),)),
        "gain": jnp.clip(1.0 + 0.18 * jax.random.normal(key_list[1], (MODEL_WIDTH,), jnp.float32), 0.1, 1.9),
        "request_adapter_index": place_ends(skewed_ids(part_splits[2], (ROWS,), ADAPTER_TOTAL, 2), jax.random.fold_in(part_splits[2], 3), 0, ADAPTER_TOTAL - 1).astype(jnp.int32),
        "lengths": draw_lengths(jax.random.fold_in(jax.random.fold_in(key_list[14], part), 71), part),
        "rotated_key_cache": draw_rotated_key_cache(jax.random.fold_in(jax.random.fold_in(key_list[14], part), 71), part),
        "earlier_value_cache": centred(part_splits[5], (ROWS, KEY_VALUE_HEADS, LMAX, HEAD_WIDTH), 1.0, 6.0, ((0, 16),)),
        "query_weight": centred(key_list[6], (MODEL_WIDTH, QUERY_HEADS * HEAD_WIDTH), MODEL_WIDTH ** -0.5, 0.0625, ((1, 8),)),
        "key_value_weight": centred(key_list[7], (MODEL_WIDTH, 2 * KEY_VALUE_HEADS * HEAD_WIDTH), MODEL_WIDTH ** -0.5, 0.0625, ((1, 8),)),
        "output_weight": centred(key_list[8], (QUERY_HEADS * HEAD_WIDTH, MODEL_WIDTH), (QUERY_HEADS * HEAD_WIDTH) ** -0.5, 0.1875, ((0, 8),)),
        "down_weight_qkv": centred(key_list[9], (MODEL_WIDTH, ADAPTER_TOTAL, 3 * ADAPTER_RANK), MODEL_WIDTH ** -0.5, 0.0625, ((0, 8), (1, 2))),
        "up_weight_query": centred(key_list[10], (ADAPTER_RANK, ADAPTER_TOTAL, QUERY_HEADS * HEAD_WIDTH), ADAPTER_RANK ** -0.5, 0.75, ((1, 2), (2, 8))),
        "up_weight_key_value": centred(key_list[11], (ADAPTER_RANK, ADAPTER_TOTAL, 2 * KEY_VALUE_HEADS * HEAD_WIDTH), ADAPTER_RANK ** -0.5, 0.75, ((1, 2), (2, 8))),
        "down_weight_output": centred(key_list[12], (QUERY_HEADS * HEAD_WIDTH, ADAPTER_TOTAL, ADAPTER_RANK), (QUERY_HEADS * HEAD_WIDTH) ** -0.5, 0.1875, ((0, 8), (1, 2))),
        "up_weight_output": centred(key_list[13], (ADAPTER_RANK, ADAPTER_TOTAL, MODEL_WIDTH), ADAPTER_RANK ** -0.5, 0.75, ((1, 2), (2, 8))),
    }


EPSILON = 1e-05

def rotate(heads_in, positions):
    half_dim = HEAD_WIDTH // 2
    frequency = 10000.0 ** (-jnp.arange(half_dim, dtype=jnp.float32) * 2.0 / HEAD_WIDTH)
    angles = positions.astype(jnp.float32)[:, None] * frequency[None, :]
    cosine = jnp.cos(angles)[:, None, :]
    sine_part = jnp.sin(angles)[:, None, :]
    first_half = heads_in[..., :half_dim]
    second_half = heads_in[..., half_dim:]
    return jnp.concatenate([first_half * cosine - second_half * sine_part, second_half * cosine + first_half * sine_part], -1)

def row_adapter_weight(left_rows, table, row_ids):
    total_rows = left_rows.shape[0]
    blocks = total_rows // 16

    def block_rows(pair):
        left_block, id_block = pair
        chosen = jnp.take(table, id_block, axis=1).astype(jnp.float32)
        return jnp.einsum('rd,drk->rk', left_block.astype(jnp.float32), chosen)
    layer_output = lax.map(block_rows, (left_rows.reshape(blocks, 16, -1), id_block_ids(row_ids, blocks)))
    return layer_output.reshape(total_rows, -1)

def id_block_ids(row_ids, blocks):
    return row_ids.reshape(blocks, 16)

def reference(hidden, gain, request_adapter_index, lengths, rotated_key_cache, earlier_value_cache, query_weight, key_value_weight, output_weight, down_weight_qkv, up_weight_query, up_weight_key_value, down_weight_output, up_weight_output):
    hidden_wide = hidden.astype(jnp.float32)
    mean_square = lax.optimization_barrier(jnp.mean(hidden_wide * hidden_wide, axis=-1, keepdims=True))
    normalized_input = (hidden_wide * lax.rsqrt(mean_square + EPSILON) * gain.astype(jnp.float32)).astype(jnp.bfloat16)
    reduced_input = row_adapter_weight(normalized_input, down_weight_qkv, request_adapter_index).astype(jnp.bfloat16)
    reduced_query = reduced_input[:, :ADAPTER_RANK]
    reduced_key = reduced_input[:, ADAPTER_RANK:2 * ADAPTER_RANK]
    reduced_value = reduced_input[:, 2 * ADAPTER_RANK:]
    query_vector = (jnp.dot(normalized_input, query_weight, preferred_element_type=jnp.float32) + row_adapter_weight(reduced_query, up_weight_query, request_adapter_index)).astype(jnp.bfloat16)
    key_value_plain = jnp.dot(normalized_input, key_value_weight, preferred_element_type=jnp.float32)
    key_column_count = KEY_VALUE_HEADS * HEAD_WIDTH
    fresh_keys = (key_value_plain[:, :key_column_count] + row_adapter_weight(reduced_key, up_weight_key_value[:, :, :key_column_count], request_adapter_index)).astype(jnp.bfloat16)
    fresh_values = (key_value_plain[:, key_column_count:] + row_adapter_weight(reduced_value, up_weight_key_value[:, :, key_column_count:], request_adapter_index)).astype(jnp.bfloat16)
    row_count = hidden.shape[0]
    group_size = QUERY_HEADS // KEY_VALUE_HEADS
    q_rot = rotate(query_vector.reshape(row_count, QUERY_HEADS, HEAD_WIDTH).astype(jnp.float32), lengths).astype(jnp.bfloat16)
    q_rot = q_rot.reshape(row_count, KEY_VALUE_HEADS, group_size, HEAD_WIDTH).astype(jnp.float32)
    k_rot = rotate(fresh_keys.reshape(row_count, KEY_VALUE_HEADS, HEAD_WIDTH).astype(jnp.float32), lengths).astype(jnp.bfloat16).astype(jnp.float32)
    values_wide = fresh_values.reshape(row_count, KEY_VALUE_HEADS, HEAD_WIDTH).astype(jnp.float32)
    score_scale = HEAD_WIDTH ** (-0.5)
    scores = jnp.einsum('rgjd,rgld->rgjl', q_rot, rotated_key_cache.astype(jnp.float32)) * score_scale
    visible = (jnp.arange(LMAX, dtype=jnp.int32)[None, :] < lengths[:, None])[:, None, None, :]
    scores = jnp.where(visible, scores, -jnp.inf)
    score_new = jnp.einsum('rgjd,rgd->rgj', q_rot, k_rot) * score_scale
    highest = jnp.maximum(lax.optimization_barrier(jnp.max(scores, axis=-1)), score_new)
    weights_cache = jnp.exp(scores - highest[..., None])
    weight_new = jnp.exp(score_new - highest)
    denominator = lax.optimization_barrier(jnp.sum(weights_cache, axis=-1)) + weight_new
    weights_cache = (weights_cache / denominator[..., None]).astype(jnp.bfloat16).astype(jnp.float32)
    weight_new = (weight_new / denominator).astype(jnp.bfloat16).astype(jnp.float32)
    attention_mixed = jnp.einsum('rgjl,rgld->rgjd', weights_cache, earlier_value_cache.astype(jnp.float32)) + weight_new[..., None] * values_wide[:, :, None, :]
    attention_mixed = attention_mixed.astype(jnp.bfloat16).reshape(row_count, QUERY_HEADS * HEAD_WIDTH)
    reduced_output = row_adapter_weight(attention_mixed, down_weight_output, request_adapter_index).astype(jnp.bfloat16)
    layer_output = jnp.dot(attention_mixed, output_weight, preferred_element_type=jnp.float32) + row_adapter_weight(reduced_output, up_weight_output, request_adapter_index)
    return layer_output.astype(jnp.bfloat16)
```

```python
import functools

import jax
import jax.numpy as jnp
from jax import lax
from jax.experimental import pallas as pl
from jax.experimental.pallas import tpu as pltpu
from jax.sharding import PartitionSpec as P

HEAD_WIDTH = 128
EPSILON = 1e-05
MESH = pl.DeviceIdType.MESH
VMEM_LIMIT = 48 * 1024 * 1024


def rotate(heads_in, positions):
    half_dim = HEAD_WIDTH // 2
    frequency = 10000.0 ** (-jnp.arange(half_dim, dtype=jnp.float32) * 2.0 / HEAD_WIDTH)
    angles = positions.astype(jnp.float32)[:, None] * frequency[None, :]
    cosine = jnp.cos(angles)[:, None, :]
    sine_part = jnp.sin(angles)[:, None, :]
    first_half = heads_in[..., :half_dim]
    second_half = heads_in[..., half_dim:]
    return jnp.concatenate(
        [
            first_half * cosine - second_half * sine_part,
            second_half * cosine + first_half * sine_part,
        ],
        -1,
    )


def pick_down(left_rows, table, onehot):
    inner_dim, slots, columns = table.shape
    product = jnp.dot(
        left_rows, table.reshape(inner_dim, slots * columns), preferred_element_type=jnp.float32
    )
    product = product.reshape(left_rows.shape[0], slots, columns)
    return jnp.sum(product * onehot[:, :, None], axis=1)


def pick_up(left_rows, table, onehot):
    rank, slots, columns = table.shape
    spread = left_rows[:, :, None] * onehot.astype(left_rows.dtype)[:, None, :]
    return jnp.dot(
        spread.reshape(left_rows.shape[0], rank * slots),
        table.reshape(rank * slots, columns),
        preferred_element_type=jnp.float32,
    )


def attend(q_rot, k_rot, fresh_values, rotated_key_cache, earlier_value_cache, lengths):
    score_scale = HEAD_WIDTH ** (-0.5)
    scores = (
        jnp.einsum("rgjd,rgld->rgjl", q_rot, rotated_key_cache, preferred_element_type=jnp.float32)
        * score_scale
    )
    cached = rotated_key_cache.shape[2]
    visible = (jnp.arange(cached, dtype=jnp.int32)[None, :] < lengths[:, None])[:, None, None, :]
    scores = jnp.where(visible, scores, -jnp.inf)
    score_new = (
        jnp.einsum("rgjd,rgd->rgj", q_rot, k_rot, preferred_element_type=jnp.float32) * score_scale
    )
    highest = jnp.maximum(jnp.max(scores, axis=-1), score_new)
    weights_cache = jnp.exp(scores - highest[..., None])
    weight_new = jnp.exp(score_new - highest)
    denominator = jnp.sum(weights_cache, axis=-1) + weight_new
    weights_cache = (weights_cache / denominator[..., None]).astype(jnp.bfloat16)
    weight_new = (weight_new / denominator).astype(jnp.bfloat16)
    mixed = jnp.einsum(
        "rgjl,rgld->rgjd", weights_cache, earlier_value_cache, preferred_element_type=jnp.float32
    )
    mixed = (
        mixed
        + weight_new.astype(jnp.float32)[..., None]
        * fresh_values.astype(jnp.float32)[:, :, None, :]
    )
    return mixed.astype(jnp.bfloat16).reshape(q_rot.shape[0], -1)


def where_am_i():
    return lax.axis_index("parts"), lax.axis_index("replica"), lax.axis_index("tensor")


def greet(peers):
    barrier = pltpu.get_barrier_semaphore()
    for peer in peers:
        pl.semaphore_signal(barrier, inc=1, device_id=peer, device_id_type=MESH)
    pl.semaphore_wait(barrier, len(peers))


def all_peers(tensor_size):
    part, replica, tensor = where_am_i()
    total = 2 * tensor_size
    me = replica * tensor_size + tensor
    found = []
    for step in range(1, total):
        other = lax.rem(me + step, total)
        found.append((other, (part, other // tensor_size, lax.rem(other, tensor_size))))
    return me, found


def tensor_peers(tensor_size):
    part, replica, tensor = where_am_i()
    found = []
    for step in range(1, tensor_size):
        other = lax.rem(tensor + step, tensor_size)
        found.append((other, (part, replica, other)))
    return tensor, found


def remote(src, dst, send, recv, peer):
    return pltpu.make_async_remote_copy(
        src_ref=src, dst_ref=dst, send_sem=send, recv_sem=recv, device_id=peer, device_id_type=MESH
    )


def exchange_kernel(tensor_size, x_ref, y_ref, send_sem, recv_sem):
    me, peers = all_peers(tensor_size)
    greet([peer for _, peer in peers])
    copies = []
    for step, (other, peer) in enumerate(peers):
        copy = remote(x_ref.at[other], y_ref.at[me], send_sem.at[step], recv_sem.at[step], peer)
        copy.start()
        copies.append(copy)
    y_ref[me] = x_ref[me]
    for copy in copies:
        copy.wait()


def call(kernel, outs, scratch, collective_id, *operands):
    return pl.pallas_call(
        kernel,
        out_shape=outs,
        in_specs=[pl.BlockSpec(memory_space=pltpu.VMEM)] * len(operands),
        out_specs=jax.tree.map(lambda _: pl.BlockSpec(memory_space=pltpu.VMEM), outs),
        scratch_shapes=scratch,
        compiler_params=pltpu.CompilerParams(
            collective_id=collective_id, has_side_effects=True, vmem_limit_bytes=VMEM_LIMIT
        ),
    )(*operands)


def exchange(x, tensor_size, collective_id):
    count = 2 * tensor_size - 1
    return call(
        functools.partial(exchange_kernel, tensor_size),
        jax.ShapeDtypeStruct(x.shape, x.dtype),
        [pltpu.SemaphoreType.DMA((count,)), pltpu.SemaphoreType.DMA((count,))],
        collective_id,
        x,
    )


def reduce_kernel(tensor_size, x_ref, y_ref, land, mine, send_a, recv_a, send_b, recv_b):
    me, peers = tensor_peers(tensor_size)
    greet([peer for _, peer in peers])
    copies = []
    for step, (other, peer) in enumerate(peers):
        copy = remote(x_ref.at[other], land.at[me], send_a.at[step], recv_a.at[step], peer)
        copy.start()
        copies.append(copy)
    land[me] = x_ref[me]
    for copy in copies:
        copy.wait()
    total = land[0]
    for step in range(1, tensor_size):
        total = total + land[step]
    mine[...] = total.astype(mine.dtype)
    copies = []
    for step, (other, peer) in enumerate(peers):
        copy = remote(mine, y_ref.at[me], send_b.at[step], recv_b.at[step], peer)
        copy.start()
        copies.append(copy)
    y_ref[me] = mine[...]
    for copy in copies:
        copy.wait()


def reduce_and_gather(x, tensor_size, collective_id):
    rows, width = x.shape
    padded = -(-width // 128) * 128
    blocks = jnp.pad(x, ((0, 0), (0, padded - width))).reshape(
        tensor_size, rows // tensor_size, padded
    )
    count = tensor_size - 1
    done = call(
        functools.partial(reduce_kernel, tensor_size),
        jax.ShapeDtypeStruct(blocks.shape, jnp.bfloat16),
        [pltpu.VMEM(blocks.shape, jnp.float32), pltpu.VMEM(blocks.shape[1:], jnp.bfloat16)]
        + [pltpu.SemaphoreType.DMA((count,))] * 4,
        collective_id,
        blocks,
    )
    return done.reshape(rows, padded)[:, :width]


def gather_kernel(
    tensor_size, x_ref, id_ref, g_ref, fo_ref, ids_ref,
    send_id, recv_id, send_up, recv_up, send_dn, recv_dn, send_y, recv_y, send_f, recv_f,
):
    part, replica, tensor = where_am_i()
    me, peers = all_peers(tensor_size)
    greet([peer for _, peer in peers])
    depth = tensor_size // 2
    level, side = tensor // 2, lax.rem(tensor, 2)
    above = (part, replica, lax.rem(tensor + 2, tensor_size))
    below = (part, replica, lax.rem(tensor + tensor_size - 2, tensor_size))
    across = (part, replica, level * 2 + 1 - side)
    twin = (part, 1 - replica, tensor)

    def block(at):
        return jnp.clip(at, 0, depth - 1) * 2 + side

    def up(step):
        at = block(level - step)
        return remote(g_ref.at[at], g_ref.at[at], send_up.at[step], recv_up.at[step], above)

    def up_in(step):
        at = block(level - step - 1)
        return remote(g_ref.at[at], g_ref.at[at], send_up.at[step], recv_up.at[step], above)

    def down(step):
        at = block(level + step)
        return remote(g_ref.at[at], g_ref.at[at], send_dn.at[step], recv_dn.at[step], below)

    def down_in(step):
        at = block(level + step + 1)
        return remote(g_ref.at[at], g_ref.at[at], send_dn.at[step], recv_dn.at[step], below)

    def cross(at_level):
        at = jnp.clip(at_level, 0, depth - 1)
        return remote(
            g_ref.at[at * 2 + side], g_ref.at[at * 2 + side], send_y.at[at], recv_y.at[at], across
        )

    def cross_in(at):
        return remote(
            g_ref.at[at * 2 + 1 - side], g_ref.at[at * 2 + 1 - side], send_y.at[at], recv_y.at[at], across
        )

    g_ref[tensor] = x_ref[...]
    has_above, has_below = level < depth - 1, level > 0

    @pl.when(has_above)
    def _():
        up(0).start()

    @pl.when(has_below)
    def _():
        down(0).start()

    cross(level).start()
    copies = []
    for step, (other, peer) in enumerate(peers):
        copy = remote(id_ref, ids_ref.at[me], send_id.at[step], recv_id.at[step], peer)
        copy.start()
        copies.append(copy)
    ids_ref[me] = id_ref[...]
    for step in range(depth - 1):

        @pl.when(level - step - 1 >= 0)
        def _():
            up_in(step).wait_recv()
            if step + 1 < depth - 1:

                @pl.when(has_above)
                def _():
                    up(step + 1).start()

            cross(level - step - 1).start()

        @pl.when(level + step + 1 < depth)
        def _():
            down_in(step).wait_recv()
            if step + 1 < depth - 1:

                @pl.when(has_below)
                def _():
                    down(step + 1).start()

            cross(level + step + 1).start()

    for at in range(depth):
        cross_in(at).wait_recv()
    swap = remote(g_ref.at[:, tensor], fo_ref, send_f, recv_f, twin)
    swap.start()
    for step in range(depth - 1):

        @pl.when(jnp.logical_and(has_above, level - step >= 0))
        def _():
            up(step).wait_send()

        @pl.when(jnp.logical_and(has_below, level + step < depth))
        def _():
            down(step).wait_send()

    for at in range(depth):
        cross(at).wait_send()
    for copy in copies:
        copy.wait()
    swap.wait()


def output_kernel(
    tensor_size, x_ref, d_ref, sum_ref, e_ref, land, send_x, recv_x, send_d, recv_d
):
    me, everyone = all_peers(tensor_size)
    tensor, peers = tensor_peers(tensor_size)
    greet([peer for _, peer in everyone])
    copies = []
    for step, (other, peer) in enumerate(peers):
        copy = remote(x_ref.at[other], land.at[tensor], send_x.at[step], recv_x.at[step], peer)
        copy.start()
        copies.append(copy)
    for step, (other, peer) in enumerate(everyone):
        copy = remote(d_ref.at[other], e_ref.at[me], send_d.at[step], recv_d.at[step], peer)
        copy.start()
        copies.append(copy)
    land[tensor] = x_ref[tensor]
    e_ref[me] = d_ref[me]
    for copy in copies:
        copy.wait()
    width = 512

    def column(at, carry):
        spot = pl.ds(pl.multiple_of(at * width, width), width)
        total = land[0, :, spot].astype(jnp.float32)
        for step in range(1, tensor_size):
            total = total + land[step, :, spot].astype(jnp.float32)
        sum_ref[:, spot] = total
        return carry

    lax.fori_loop(0, sum_ref.shape[1] // width, column, 0)


def fold_slices(rows, slices):
    count, width = rows.shape
    part = width // slices // 2
    return rows.reshape(count, slices, 2, part).transpose(1, 0, 2, 3).reshape(slices, 2 * count, part)


def shards(
    hidden,
    gain,
    request_adapter_index,
    lengths,
    rotated_key_cache,
    earlier_value_cache,
    query_weight,
    key_value_weight,
    output_weight,
    down_weight_qkv,
    up_weight_query,
    up_weight_key_value,
    down_weight_output,
    up_weight_output,
):
    tensor_at = lax.axis_index("tensor")
    size = lax.axis_size("tensor")
    replica_at = lax.axis_index("replica")
    own_rows, model_width = hidden.shape
    batch_rows = own_rows * size
    every_row = 2 * batch_rows
    hidden_wide = hidden.astype(jnp.float32)
    mean_square = jnp.mean(hidden_wide * hidden_wide, axis=-1, keepdims=True)
    normalized_input = (hidden_wide * lax.rsqrt(mean_square + EPSILON) * gain).astype(jnp.bfloat16)

    folded = fold_slices(normalized_input, size)
    half = folded.shape[2]
    id_tile = jnp.broadcast_to(request_adapter_index[:, None], (own_rows, 128))
    depth = size // 2
    dma = pltpu.SemaphoreType.DMA
    steps = max(depth - 1, 1)
    gathered, other_features, id_tiles = call(
        functools.partial(gather_kernel, size),
        (
            jax.ShapeDtypeStruct((size,) + folded.shape, jnp.bfloat16),
            jax.ShapeDtypeStruct(folded.shape, jnp.bfloat16),
            jax.ShapeDtypeStruct((2 * size, own_rows, 128), jnp.int32),
        ),
        [dma((2 * size - 1,)), dma((2 * size - 1,))] + [dma((steps,))] * 4 + [dma((depth,))] * 2
        + [dma, dma],
        0,
        folded,
        id_tile,
    )
    own_features = lax.dynamic_index_in_dim(gathered, tensor_at, 1, keepdims=False)

    def unfold(blocks):
        return (
            blocks.reshape(size, own_rows, 2, half).reshape(batch_rows, 2 * half)
        )

    own_features, other_features = unfold(own_features), unfold(other_features)
    features = jnp.where(
        replica_at == 0,
        jnp.concatenate([own_features, other_features], 0),
        jnp.concatenate([other_features, own_features], 0),
    )
    full = (
        gathered.reshape(size, size, own_rows, 2, half)
        .transpose(0, 2, 1, 3, 4)
        .reshape(batch_rows, model_width)
    )
    every_id = id_tiles[:, :, 0].reshape(every_row)
    slots = down_weight_qkv.shape[1]
    onehot = (
        (every_id - replica_at * slots)[:, None] == jnp.arange(slots, dtype=jnp.int32)[None, :]
    ).astype(jnp.float32)
    reduced_input = reduce_and_gather(pick_down(features, down_weight_qkv, onehot), size, 1)
    base = jnp.concatenate(
        [
            jnp.dot(full, query_weight, preferred_element_type=jnp.float32),
            jnp.dot(full, key_value_weight, preferred_element_type=jnp.float32),
        ],
        1,
    )
    rank_size = up_weight_query.shape[0]
    shrink_kv = jnp.where(
        tensor_at < size // 2,
        reduced_input[:, rank_size : 2 * rank_size],
        reduced_input[:, 2 * rank_size :],
    )
    delta = jnp.concatenate(
        [
            pick_up(reduced_input[:, :rank_size], up_weight_query, onehot),
            pick_up(shrink_kv, up_weight_key_value, onehot),
        ],
        1,
    ).reshape(2, batch_rows, -1)
    own = (jnp.arange(2) == replica_at)[:, None, None]
    delta = delta + jnp.where(own, base[None], 0.0)
    query_cols = query_weight.shape[1]
    kv_cols = key_value_weight.shape[1]
    padded = -(-(query_cols + kv_cols) // 128) * 128
    delta = jnp.pad(delta, ((0, 0), (0, 0), (0, padded - query_cols - kv_cols)))
    arrived = exchange(delta.reshape(2 * size, own_rows, padded), size, 2)
    arrived = arrived.reshape(2, size, own_rows, padded)
    arrived = (arrived[0] + arrived[1]).astype(jnp.bfloat16).transpose(1, 0, 2)
    query_rows = arrived[:, :, :query_cols].reshape(own_rows, size * query_cols)
    kv_rows = arrived[:, :, query_cols : query_cols + kv_cols].reshape(own_rows, size * kv_cols)
    head_count = query_rows.shape[1] // HEAD_WIDTH
    kv_heads = kv_rows.shape[1] // (2 * HEAD_WIDTH)
    q_rot = rotate(
        query_rows.reshape(own_rows, head_count, HEAD_WIDTH).astype(jnp.float32), lengths
    ).astype(jnp.bfloat16)
    q_rot = q_rot.reshape(own_rows, kv_heads, head_count // kv_heads, HEAD_WIDTH)
    k_rot = rotate(
        kv_rows[:, : kv_heads * HEAD_WIDTH]
        .reshape(own_rows, kv_heads, HEAD_WIDTH)
        .astype(jnp.float32),
        lengths,
    ).astype(jnp.bfloat16)
    fresh_values = kv_rows[:, kv_heads * HEAD_WIDTH :].reshape(own_rows, kv_heads, HEAD_WIDTH)
    mixed = attend(q_rot, k_rot, fresh_values, rotated_key_cache, earlier_value_cache, lengths)
    head_cols = mixed.shape[1] // size
    leaving = mixed.astype(jnp.float32).reshape(own_rows, size, head_cols).transpose(1, 0, 2)
    heads = exchange(jnp.concatenate([leaving, leaving], 0), size, 3)
    heads = heads.reshape(every_row, head_cols).astype(jnp.bfloat16)
    reduced_output = reduce_and_gather(pick_down(heads, down_weight_output, onehot), size, 4)
    delta_out = pick_up(reduced_output, up_weight_output, onehot).astype(jnp.bfloat16)
    out_cols = delta_out.shape[1]
    own_heads = lax.dynamic_slice_in_dim(heads, replica_at * batch_rows, batch_rows)
    term = jnp.dot(own_heads, output_weight, preferred_element_type=jnp.float32).astype(jnp.bfloat16)
    pieces = term.reshape(size, own_rows, 2, model_width // 2).transpose(0, 2, 1, 3)
    pieces = pieces.reshape(size, 2 * own_rows, model_width // 2)
    deltas = delta_out.reshape(2 * size, own_rows, 2, out_cols // 2).transpose(0, 2, 1, 3)
    deltas = deltas.reshape(2 * size, 2 * own_rows, out_cols // 2)
    total, extra = call(
        functools.partial(output_kernel, size),
        (
            jax.ShapeDtypeStruct(pieces.shape[1:], jnp.float32),
            jax.ShapeDtypeStruct(deltas.shape, jnp.bfloat16),
        ),
        [pltpu.VMEM(pieces.shape, jnp.bfloat16)]
        + [dma((size - 1,))] * 2
        + [dma((2 * size - 1,))] * 2,
        5,
        pieces,
        deltas,
    )
    total = total.reshape(2, own_rows, model_width // 2).transpose(1, 0, 2).reshape(own_rows, model_width)
    extra = extra.reshape(2, size, 2, own_rows, out_cols // 2).astype(jnp.float32)
    extra = (extra[0] + extra[1]).transpose(2, 0, 1, 3).reshape(own_rows, model_width)
    return (total + extra).astype(jnp.bfloat16)


def solution(mesh):
    return jax.shard_map(
        shards,
        mesh=mesh,
        in_specs=(
            P(("parts", "replica", "tensor"), None),
            P(),
            P(("parts", "replica", "tensor")),
            P(("parts", "replica", "tensor")),
            P(("parts", "replica", "tensor"), None, None, None),
            P(("parts", "replica", "tensor"), None, None, None),
            P(None, "tensor"),
            P(None, "tensor"),
            P("tensor", None),
            P("tensor", "replica", None),
            P(None, "replica", "tensor"),
            P(None, "replica", "tensor"),
            P("tensor", "replica", None),
            P(None, "replica", "tensor"),
        ),
        out_specs=P(("parts", "replica", "tensor"), None),
        check_vma=False,
    )
```

```python
import functools

import jax
import jax.numpy as jnp
from jax import lax
from jax.experimental import pallas as pl
from jax.experimental.pallas import tpu as pltpu
from jax.sharding import PartitionSpec as P

HEAD_WIDTH = 128
EPSILON = 1e-05
MESH = pl.DeviceIdType.MESH
VMEM_LIMIT = 48 * 1024 * 1024


def rotate(heads_in, positions):
    half_dim = HEAD_WIDTH // 2
    frequency = 10000.0 ** (-jnp.arange(half_dim, dtype=jnp.float32) * 2.0 / HEAD_WIDTH)
    angles = positions.astype(jnp.float32)[:, None] * frequency[None, :]
    cosine = jnp.cos(angles)[:, None, :]
    sine_part = jnp.sin(angles)[:, None, :]
    first_half = heads_in[..., :half_dim]
    second_half = heads_in[..., half_dim:]
    return jnp.concatenate(
        [
            first_half * cosine - second_half * sine_part,
            second_half * cosine + first_half * sine_part,
        ],
        -1,
    )


def pick_down(left_rows, table, onehot):
    inner_dim, slots, columns = table.shape
    product = jnp.dot(
        left_rows, table.reshape(inner_dim, slots * columns), preferred_element_type=jnp.float32
    )
    product = product.reshape(left_rows.shape[0], slots, columns)
    return jnp.sum(product * onehot[:, :, None], axis=1)


def pick_up(left_rows, table, onehot):
    rank, slots, columns = table.shape
    spread = left_rows[:, :, None] * onehot.astype(left_rows.dtype)[:, None, :]
    return jnp.dot(
        spread.reshape(left_rows.shape[0], rank * slots),
        table.reshape(rank * slots, columns),
        preferred_element_type=jnp.float32,
    )


def attend(q_rot, k_rot, fresh_values, rotated_key_cache, earlier_value_cache, lengths):
    score_scale = HEAD_WIDTH ** (-0.5)
    scores = (
        jnp.einsum("rgjd,rgld->rgjl", q_rot, rotated_key_cache, preferred_element_type=jnp.float32)
        * score_scale
    )
    cached = rotated_key_cache.shape[2]
    visible = (jnp.arange(cached, dtype=jnp.int32)[None, :] < lengths[:, None])[:, None, None, :]
    scores = jnp.where(visible, scores, -jnp.inf)
    score_new = (
        jnp.einsum("rgjd,rgd->rgj", q_rot, k_rot, preferred_element_type=jnp.float32) * score_scale
    )
    highest = jnp.maximum(jnp.max(scores, axis=-1), score_new)
    weights_cache = jnp.exp(scores - highest[..., None])
    weight_new = jnp.exp(score_new - highest)
    denominator = jnp.sum(weights_cache, axis=-1) + weight_new
    weights_cache = (weights_cache / denominator[..., None]).astype(jnp.bfloat16)
    weight_new = (weight_new / denominator).astype(jnp.bfloat16)
    mixed = jnp.einsum(
        "rgjl,rgld->rgjd", weights_cache, earlier_value_cache, preferred_element_type=jnp.float32
    )
    mixed = (
        mixed
        + weight_new.astype(jnp.float32)[..., None]
        * fresh_values.astype(jnp.float32)[:, :, None, :]
    )
    return mixed.astype(jnp.bfloat16).reshape(q_rot.shape[0], -1)


def where_am_i():
    return lax.axis_index("parts"), lax.axis_index("replica"), lax.axis_index("tensor")


def greet(peers):
    barrier = pltpu.get_barrier_semaphore()
    for peer in peers:
        pl.semaphore_signal(barrier, inc=1, device_id=peer, device_id_type=MESH)
    pl.semaphore_wait(barrier, len(peers))


def all_peers(tensor_size):
    part, replica, tensor = where_am_i()
    total = 2 * tensor_size
    me = replica * tensor_size + tensor
    found = []
    for step in range(1, total):
        other = lax.rem(me + step, total)
        found.append((other, (part, other // tensor_size, lax.rem(other, tensor_size))))
    return me, found


def tensor_peers(tensor_size):
    part, replica, tensor = where_am_i()
    found = []
    for step in range(1, tensor_size):
        other = lax.rem(tensor + step, tensor_size)
        found.append((other, (part, replica, other)))
    return tensor, found


def remote(src, dst, send, recv, peer):
    return pltpu.make_async_remote_copy(
        src_ref=src, dst_ref=dst, send_sem=send, recv_sem=recv, device_id=peer, device_id_type=MESH
    )


def exchange_kernel(tensor_size, x_ref, y_ref, send_sem, recv_sem):
    me, peers = all_peers(tensor_size)
    greet([peer for _, peer in peers])
    copies = []
    for step, (other, peer) in enumerate(peers):
        copy = remote(x_ref.at[other], y_ref.at[me], send_sem.at[step], recv_sem.at[step], peer)
        copy.start()
        copies.append(copy)
    y_ref[me] = x_ref[me]
    for copy in copies:
        copy.wait()


def call(kernel, outs, scratch, collective_id, *operands):
    return pl.pallas_call(
        kernel,
        out_shape=outs,
        in_specs=[pl.BlockSpec(memory_space=pltpu.VMEM)] * len(operands),
        out_specs=jax.tree.map(lambda _: pl.BlockSpec(memory_space=pltpu.VMEM), outs),
        scratch_shapes=scratch,
        compiler_params=pltpu.CompilerParams(
            collective_id=collective_id, has_side_effects=True, vmem_limit_bytes=VMEM_LIMIT
        ),
    )(*operands)


def exchange(x, tensor_size, collective_id):
    count = 2 * tensor_size - 1
    return call(
        functools.partial(exchange_kernel, tensor_size),
        jax.ShapeDtypeStruct(x.shape, x.dtype),
        [pltpu.SemaphoreType.DMA((count,)), pltpu.SemaphoreType.DMA((count,))],
        collective_id,
        x,
    )


def reduce_kernel(tensor_size, x_ref, y_ref, land, mine, send_a, recv_a, send_b, recv_b):
    me, peers = tensor_peers(tensor_size)
    greet([peer for _, peer in peers])
    copies = []
    for step, (other, peer) in enumerate(peers):
        copy = remote(x_ref.at[other], land.at[me], send_a.at[step], recv_a.at[step], peer)
        copy.start()
        copies.append(copy)
    land[me] = x_ref[me]
    for copy in copies:
        copy.wait()
    total = land[0]
    for step in range(1, tensor_size):
        total = total + land[step]
    mine[...] = total.astype(mine.dtype)
    copies = []
    for step, (other, peer) in enumerate(peers):
        copy = remote(mine, y_ref.at[me], send_b.at[step], recv_b.at[step], peer)
        copy.start()
        copies.append(copy)
    y_ref[me] = mine[...]
    for copy in copies:
        copy.wait()


def reduce_and_gather(x, tensor_size, collective_id):
    rows, width = x.shape
    padded = -(-width // 128) * 128
    blocks = jnp.pad(x, ((0, 0), (0, padded - width))).reshape(
        tensor_size, rows // tensor_size, padded
    )
    count = tensor_size - 1
    done = call(
        functools.partial(reduce_kernel, tensor_size),
        jax.ShapeDtypeStruct(blocks.shape, jnp.bfloat16),
        [pltpu.VMEM(blocks.shape, jnp.float32), pltpu.VMEM(blocks.shape[1:], jnp.bfloat16)]
        + [pltpu.SemaphoreType.DMA((count,))] * 4,
        collective_id,
        blocks,
    )
    return done.reshape(rows, padded)[:, :width]


def gather_kernel(
    tensor_size, x_ref, id_ref, g_ref, fo_ref, ids_ref,
    send_id, recv_id, send_up, recv_up, send_dn, recv_dn, send_y, recv_y, send_f, recv_f,
):
    part, replica, tensor = where_am_i()
    me, peers = all_peers(tensor_size)
    greet([peer for _, peer in peers])
    depth = tensor_size // 2
    level, side = tensor // 2, lax.rem(tensor, 2)
    above = (part, replica, lax.rem(tensor + 2, tensor_size))
    below = (part, replica, lax.rem(tensor + tensor_size - 2, tensor_size))
    across = (part, replica, level * 2 + 1 - side)
    twin = (part, 1 - replica, tensor)

    def block(at):
        return jnp.clip(at, 0, depth - 1) * 2 + side

    def up(step):
        at = block(level - step)
        return remote(g_ref.at[at], g_ref.at[at], send_up.at[step], recv_up.at[step], above)

    def up_in(step):
        at = block(level - step - 1)
        return remote(g_ref.at[at], g_ref.at[at], send_up.at[step], recv_up.at[step], above)

    def down(step):
        at = block(level + step)
        return remote(g_ref.at[at], g_ref.at[at], send_dn.at[step], recv_dn.at[step], below)

    def down_in(step):
        at = block(level + step + 1)
        return remote(g_ref.at[at], g_ref.at[at], send_dn.at[step], recv_dn.at[step], below)

    def cross(at_level):
        at = jnp.clip(at_level, 0, depth - 1)
        return remote(
            g_ref.at[at * 2 + side], g_ref.at[at * 2 + side], send_y.at[at], recv_y.at[at], across
        )

    def cross_in(at):
        return remote(
            g_ref.at[at * 2 + 1 - side], g_ref.at[at * 2 + 1 - side], send_y.at[at], recv_y.at[at], across
        )

    g_ref[tensor] = x_ref[...]
    has_above, has_below = level < depth - 1, level > 0

    @pl.when(has_above)
    def _():
        up(0).start()

    @pl.when(has_below)
    def _():
        down(0).start()

    cross(level).start()
    copies = []
    for step, (other, peer) in enumerate(peers):
        copy = remote(id_ref, ids_ref.at[me], send_id.at[step], recv_id.at[step], peer)
        copy.start()
        copies.append(copy)
    ids_ref[me] = id_ref[...]
    for step in range(depth - 1):

        @pl.when(level - step - 1 >= 0)
        def _():
            up_in(step).wait_recv()
            if step + 1 < depth - 1:

                @pl.when(has_above)
                def _():
                    up(step + 1).start()

            cross(level - step - 1).start()

        @pl.when(level + step + 1 < depth)
        def _():
            down_in(step).wait_recv()
            if step + 1 < depth - 1:

                @pl.when(has_below)
                def _():
                    down(step + 1).start()

            cross(level + step + 1).start()

    for at in range(depth):
        cross_in(at).wait_recv()
    swap = remote(g_ref.at[:, tensor], fo_ref, send_f, recv_f, twin)
    swap.start()
    for step in range(depth - 1):

        @pl.when(jnp.logical_and(has_above, level - step >= 0))
        def _():
            up(step).wait_send()

        @pl.when(jnp.logical_and(has_below, level + step < depth))
        def _():
            down(step).wait_send()

    for at in range(depth):
        cross(at).wait_send()
    for copy in copies:
        copy.wait()
    swap.wait()


def tail_kernel(
    size, chunks, rank, ids_ref, x_ref, ao_hbm, wo_hbm, bo_hbm, out_ref,
    ao, wo, bo, heads_in, red_x, red_land, red_mine, red_all, spread,
    near, away, land_y, land_z, d_out, d_in,
    load, send_h, recv_h, send_a, recv_a, send_b, recv_b, send_d, recv_d,
    send_y, recv_y, send_z, recv_z,
):
    part, replica, tensor = where_am_i()
    loads = [
        pltpu.make_async_copy(src, dst, load.at[at])
        for at, (src, dst) in enumerate(((ao_hbm, ao), (wo_hbm, wo), (bo_hbm, bo)))
    ]
    for copy in loads:
        copy.start()
    me, everyone = all_peers(size)
    _, peers = tensor_peers(size)
    greet([peer for _, peer in everyone])
    depth = size // 2
    level, side = tensor // 2, lax.rem(tensor, 2)
    across = (part, replica, level * 2 + 1 - side)
    rows = heads_in.shape[1]
    batch = rows * size
    every = 2 * batch
    model = out_ref.shape[1]
    half = model // 2
    slots = bo.shape[0] // rank

    sent = []
    for step, (other, peer) in enumerate(everyone):
        copy = remote(
            x_ref.at[lax.rem(other, size)], heads_in.at[me], send_h.at[step], recv_h.at[step], peer
        )
        copy.start()
        sent.append(copy)
    heads_in[me] = x_ref[tensor]
    for copy in sent:
        copy.wait()
    heads = heads_in[...].reshape(every, heads_in.shape[2]).astype(jnp.bfloat16)
    local_id = ids_ref[:, :1] - replica * slots
    loads[0].wait()
    wide = 512
    total = None
    for at in range(0, ao.shape[0], wide):
        product = lax.dot_general(
            heads, ao[at : at + wide, :], (((1,), (1,)), ((), ())), preferred_element_type=jnp.float32
        )
        first = lax.broadcasted_iota(jnp.int32, product.shape, 1) + at - local_id * rank
        product = jnp.where(jnp.logical_and(first >= 0, first < rank), product, 0.0)
        for lane in range(0, wide, 128):
            piece = product[:, lane : lane + 128]
            total = piece if total is None else total + piece
    if rank == 64:
        total = total + pltpu.roll(total, 64, 1)
    red_x[...] = total.reshape(red_x.shape)
    sent = []
    for step, (other, peer) in enumerate(peers):
        copy = remote(red_x.at[other], red_land.at[tensor], send_a.at[step], recv_a.at[step], peer)
        copy.start()
        sent.append(copy)
    red_land[tensor] = red_x[tensor]

    own = heads_in[pl.ds(replica * size, size)].reshape(batch, heads_in.shape[2]).astype(jnp.bfloat16)
    loads[1].wait()
    width = half // chunks
    y_copies = []
    for chunk in range(chunks):
        parts = []
        for start in (chunk * width, half + chunk * width):
            term = jnp.dot(own, wo[:, start : start + width], preferred_element_type=jnp.float32)
            parts.append(term.reshape(size, rows, width))
        term = jnp.concatenate(parts, 1).reshape(depth, 2, 2 * rows, width)
        here = jnp.where(side == 0, term[:, 0], term[:, 1])
        there = jnp.where(side == 0, term[:, 1], term[:, 0])
        away[chunk] = there.astype(jnp.bfloat16)
        copy = remote(away.at[chunk], land_y.at[chunk], send_y.at[chunk], recv_y.at[chunk], across)
        copy.start()
        y_copies.append(copy)
        near[chunk] = here

    for copy in sent:
        copy.wait()
    total = red_land[0]
    for step in range(1, size):
        total = total + red_land[step]
    red_mine[...] = total.astype(jnp.bfloat16)
    sent = []
    for step, (other, peer) in enumerate(peers):
        copy = remote(red_mine, red_all.at[tensor], send_b.at[step], recv_b.at[step], peer)
        copy.start()
        sent.append(copy)
    red_all[tensor] = red_mine[...]

    z_copies = []

    def pass_on(chunk):
        y_copies[chunk].wait()
        near[chunk] = near[chunk] + land_y[chunk].astype(jnp.float32)
        away[chunk] = near[chunk].astype(jnp.bfloat16)
        for step in range(1, depth):
            other = lax.rem(level + step, depth)
            copy = remote(
                away.at[chunk, other], land_z.at[chunk, level],
                send_z.at[chunk, step - 1], recv_z.at[chunk, step - 1],
                (part, replica, other * 2 + side),
            )
            copy.start()
            z_copies.append(copy)
        land_z[chunk, level] = away[chunk, level]

    early = min(1, chunks)
    for chunk in range(early):
        pass_on(chunk)
    for copy in sent:
        copy.wait()
    shrunk = red_all[...].reshape(every, red_all.shape[2])
    for at in range(0, bo.shape[0], wide):
        shape = (shrunk.shape[1], wide)
        place = lax.broadcasted_iota(jnp.int32, shape, 1) + at
        place = place - lax.broadcasted_iota(jnp.int32, shape, 0) * slots
        expand = jnp.where(jnp.logical_and(place >= 0, place < slots), 1.0, 0.0).astype(jnp.bfloat16)
        piece = jnp.dot(shrunk, expand, preferred_element_type=jnp.float32)
        slot = lax.rem(lax.broadcasted_iota(jnp.int32, piece.shape, 1), slots)
        spread[:, at : at + wide] = jnp.where(slot == local_id, piece, 0.0).astype(jnp.bfloat16)
    loads[2].wait()
    cols = bo.shape[1]
    delta = jnp.concatenate(
        [
            jnp.dot(
                spread[...], bo[:, at : at + cols // 2], preferred_element_type=jnp.float32
            ).reshape(2 * size, rows, cols // 2)
            for at in (0, cols // 2)
        ],
        1,
    )
    d_out[...] = delta.astype(jnp.bfloat16)
    d_copies = []
    for step, (other, peer) in enumerate(everyone):
        copy = remote(d_out.at[other], d_in.at[me], send_d.at[step], recv_d.at[step], peer)
        copy.start()
        d_copies.append(copy)
    d_in[me] = d_out[me]
    for chunk in range(early, chunks):
        pass_on(chunk)
    count = depth - 1
    for chunk in range(chunks):
        for copy in z_copies[chunk * count : (chunk + 1) * count]:
            copy.wait()
        total = land_z[chunk, 0].astype(jnp.float32)
        for at in range(1, depth):
            total = total + land_z[chunk, at].astype(jnp.float32)
        out_ref[:, chunk * width : (chunk + 1) * width] = total[:rows]
        out_ref[:, half + chunk * width : half + (chunk + 1) * width] = total[rows:]
    for copy in d_copies:
        copy.wait()
    for at in range(size):
        extra = d_in[at].astype(jnp.float32) + d_in[size + at].astype(jnp.float32)
        start = at * cols
        out_ref[:, start : start + cols // 2] += extra[:rows]
        out_ref[:, start + cols // 2 : start + cols] += extra[rows:]


def fold_slices(rows, slices):
    count, width = rows.shape
    part = width // slices // 2
    return rows.reshape(count, slices, 2, part).transpose(1, 0, 2, 3).reshape(slices, 2 * count, part)


def shards(
    hidden,
    gain,
    request_adapter_index,
    lengths,
    rotated_key_cache,
    earlier_value_cache,
    query_weight,
    key_value_weight,
    output_weight,
    down_weight_qkv,
    up_weight_query,
    up_weight_key_value,
    down_weight_output,
    up_weight_output,
):
    tensor_at = lax.axis_index("tensor")
    size = lax.axis_size("tensor")
    replica_at = lax.axis_index("replica")
    own_rows, model_width = hidden.shape
    batch_rows = own_rows * size
    every_row = 2 * batch_rows
    hidden_wide = hidden.astype(jnp.float32)
    mean_square = jnp.mean(hidden_wide * hidden_wide, axis=-1, keepdims=True)
    normalized_input = (hidden_wide * lax.rsqrt(mean_square + EPSILON) * gain).astype(jnp.bfloat16)

    folded = fold_slices(normalized_input, size)
    half = folded.shape[2]
    id_tile = jnp.broadcast_to(request_adapter_index[:, None], (own_rows, 128))
    depth = size // 2
    dma = pltpu.SemaphoreType.DMA
    steps = max(depth - 1, 1)
    gathered, other_features, id_tiles = call(
        functools.partial(gather_kernel, size),
        (
            jax.ShapeDtypeStruct((size,) + folded.shape, jnp.bfloat16),
            jax.ShapeDtypeStruct(folded.shape, jnp.bfloat16),
            jax.ShapeDtypeStruct((2 * size, own_rows, 128), jnp.int32),
        ),
        [dma((2 * size - 1,)), dma((2 * size - 1,))] + [dma((steps,))] * 4 + [dma((depth,))] * 2
        + [dma, dma],
        0,
        folded,
        id_tile,
    )
    own_features = lax.dynamic_index_in_dim(gathered, tensor_at, 1, keepdims=False)

    def unfold(blocks):
        return (
            blocks.reshape(size, own_rows, 2, half).reshape(batch_rows, 2 * half)
        )

    own_features, other_features = unfold(own_features), unfold(other_features)
    features = jnp.where(
        replica_at == 0,
        jnp.concatenate([own_features, other_features], 0),
        jnp.concatenate([other_features, own_features], 0),
    )
    full = (
        gathered.reshape(size, size, own_rows, 2, half)
        .transpose(0, 2, 1, 3, 4)
        .reshape(batch_rows, model_width)
    )
    every_id = id_tiles[:, :, 0].reshape(every_row)
    slots = down_weight_qkv.shape[1]
    onehot = (
        (every_id - replica_at * slots)[:, None] == jnp.arange(slots, dtype=jnp.int32)[None, :]
    ).astype(jnp.float32)
    reduced_input = reduce_and_gather(pick_down(features, down_weight_qkv, onehot), size, 1)
    base = jnp.concatenate(
        [
            jnp.dot(full, query_weight, preferred_element_type=jnp.float32),
            jnp.dot(full, key_value_weight, preferred_element_type=jnp.float32),
        ],
        1,
    )
    rank_size = up_weight_query.shape[0]
    shrink_kv = jnp.where(
        tensor_at < size // 2,
        reduced_input[:, rank_size : 2 * rank_size],
        reduced_input[:, 2 * rank_size :],
    )
    delta = jnp.concatenate(
        [
            pick_up(reduced_input[:, :rank_size], up_weight_query, onehot),
            pick_up(shrink_kv, up_weight_key_value, onehot),
        ],
        1,
    ).reshape(2, batch_rows, -1)
    own = (jnp.arange(2) == replica_at)[:, None, None]
    delta = delta + jnp.where(own, base[None], 0.0)
    query_cols = query_weight.shape[1]
    kv_cols = key_value_weight.shape[1]
    padded = -(-(query_cols + kv_cols) // 128) * 128
    delta = jnp.pad(delta, ((0, 0), (0, 0), (0, padded - query_cols - kv_cols)))
    arrived = exchange(delta.reshape(2 * size, own_rows, padded), size, 2)
    arrived = arrived.reshape(2, size, own_rows, padded)
    arrived = (arrived[0] + arrived[1]).astype(jnp.bfloat16).transpose(1, 0, 2)
    query_rows = arrived[:, :, :query_cols].reshape(own_rows, size * query_cols)
    kv_rows = arrived[:, :, query_cols : query_cols + kv_cols].reshape(own_rows, size * kv_cols)
    head_count = query_rows.shape[1] // HEAD_WIDTH
    kv_heads = kv_rows.shape[1] // (2 * HEAD_WIDTH)
    q_rot = rotate(
        query_rows.reshape(own_rows, head_count, HEAD_WIDTH).astype(jnp.float32), lengths
    ).astype(jnp.bfloat16)
    q_rot = q_rot.reshape(own_rows, kv_heads, head_count // kv_heads, HEAD_WIDTH)
    k_rot = rotate(
        kv_rows[:, : kv_heads * HEAD_WIDTH]
        .reshape(own_rows, kv_heads, HEAD_WIDTH)
        .astype(jnp.float32),
        lengths,
    ).astype(jnp.bfloat16)
    fresh_values = kv_rows[:, kv_heads * HEAD_WIDTH :].reshape(own_rows, kv_heads, HEAD_WIDTH)
    mixed = attend(q_rot, k_rot, fresh_values, rotated_key_cache, earlier_value_cache, lengths)
    head_cols = mixed.shape[1] // size
    leaving = mixed.astype(jnp.float32).reshape(own_rows, size, head_cols).transpose(1, 0, 2)
    rank_out, _, out_cols = up_weight_output.shape
    down_table = down_weight_output.transpose(1, 2, 0).reshape(-1, head_cols)
    up_table = up_weight_output.reshape(rank_out * slots, out_cols)
    chunks = 4
    width = model_width // 2 // chunks
    double = 2 * own_rows
    vmem, f32, bf16 = pltpu.VMEM, jnp.float32, jnp.bfloat16
    out = pl.pallas_call(
        functools.partial(tail_kernel, size, chunks, rank_out),
        out_shape=jax.ShapeDtypeStruct((own_rows, model_width), f32),
        in_specs=[pl.BlockSpec(memory_space=vmem)] * 2 + [pl.BlockSpec(memory_space=pl.ANY)] * 3,
        out_specs=pl.BlockSpec(memory_space=vmem),
        scratch_shapes=[
            vmem(down_table.shape, bf16),
            vmem(output_weight.shape, bf16),
            vmem(up_table.shape, bf16),
            vmem((2 * size, own_rows, head_cols), f32),
            vmem((size, double, 128), f32),
            vmem((size, double, 128), f32),
            vmem((double, 128), bf16),
            vmem((size, double, 128), bf16),
            vmem((every_row, rank_out * slots), bf16),
            vmem((chunks, depth, double, width), f32),
            vmem((chunks, depth, double, width), bf16),
            vmem((chunks, depth, double, width), bf16),
            vmem((chunks, depth, double, width), bf16),
            vmem((2 * size, double, out_cols // 2), bf16),
            vmem((2 * size, double, out_cols // 2), bf16),
            dma((3,)),
            dma((2 * size - 1,)),
            dma((2 * size - 1,)),
            dma((size - 1,)),
            dma((size - 1,)),
            dma((size - 1,)),
            dma((size - 1,)),
            dma((2 * size - 1,)),
            dma((2 * size - 1,)),
            dma((chunks,)),
            dma((chunks,)),
            dma((chunks, steps)),
            dma((chunks, steps)),
        ],
        compiler_params=pltpu.CompilerParams(
            collective_id=3, has_side_effects=True, vmem_limit_bytes=VMEM_LIMIT
        ),
    )(id_tiles.reshape(every_row, 128), leaving, down_table, output_weight, up_table)
    return out.astype(jnp.bfloat16)


def solution(mesh):
    return jax.shard_map(
        shards,
        mesh=mesh,
        in_specs=(
            P(("parts", "replica", "tensor"), None),
            P(),
            P(("parts", "replica", "tensor")),
            P(("parts", "replica", "tensor")),
            P(("parts", "replica", "tensor"), None, None, None),
            P(("parts", "replica", "tensor"), None, None, None),
            P(None, "tensor"),
            P(None, "tensor"),
            P("tensor", None),
            P("tensor", "replica", None),
            P(None, "replica", "tensor"),
            P(None, "replica", "tensor"),
            P("tensor", "replica", None),
            P(None, "replica", "tensor"),
        ),
        out_specs=P(("parts", "replica", "tensor"), None),
        check_vma=False,
    )
```

```python
import functools

import jax
import jax.numpy as jnp
from jax import lax
from jax.experimental import pallas as pl
from jax.experimental.pallas import tpu as pltpu
from jax.sharding import PartitionSpec as P

HEAD_WIDTH = 128
EPSILON = 1e-05
MESH = pl.DeviceIdType.MESH
VMEM_LIMIT = 48 * 1024 * 1024


def rotate(heads_in, positions):
    half_dim = HEAD_WIDTH // 2
    frequency = 10000.0 ** (-jnp.arange(half_dim, dtype=jnp.float32) * 2.0 / HEAD_WIDTH)
    angles = positions.astype(jnp.float32)[:, None] * frequency[None, :]
    cosine = jnp.cos(angles)[:, None, :]
    sine_part = jnp.sin(angles)[:, None, :]
    first_half = heads_in[..., :half_dim]
    second_half = heads_in[..., half_dim:]
    return jnp.concatenate(
        [
            first_half * cosine - second_half * sine_part,
            second_half * cosine + first_half * sine_part,
        ],
        -1,
    )


def attend(q_rot, k_rot, fresh_values, rotated_key_cache, earlier_value_cache, lengths):
    score_scale = HEAD_WIDTH ** (-0.5)
    scores = (
        jnp.einsum("rgjd,rgld->rgjl", q_rot, rotated_key_cache, preferred_element_type=jnp.float32)
        * score_scale
    )
    cached = rotated_key_cache.shape[2]
    visible = (jnp.arange(cached, dtype=jnp.int32)[None, :] < lengths[:, None])[:, None, None, :]
    scores = jnp.where(visible, scores, -jnp.inf)
    score_new = (
        jnp.einsum("rgjd,rgd->rgj", q_rot, k_rot, preferred_element_type=jnp.float32) * score_scale
    )
    highest = jnp.maximum(jnp.max(scores, axis=-1), score_new)
    weights_cache = jnp.exp(scores - highest[..., None])
    weight_new = jnp.exp(score_new - highest)
    denominator = jnp.sum(weights_cache, axis=-1) + weight_new
    weights_cache = (weights_cache / denominator[..., None]).astype(jnp.bfloat16)
    weight_new = (weight_new / denominator).astype(jnp.bfloat16)
    mixed = jnp.einsum(
        "rgjl,rgld->rgjd", weights_cache, earlier_value_cache, preferred_element_type=jnp.float32
    )
    mixed = (
        mixed
        + weight_new.astype(jnp.float32)[..., None]
        * fresh_values.astype(jnp.float32)[:, :, None, :]
    )
    return mixed.astype(jnp.bfloat16).reshape(q_rot.shape[0], -1)


def where_am_i():
    return lax.axis_index("parts"), lax.axis_index("replica"), lax.axis_index("tensor")


def greet(peers):
    barrier = pltpu.get_barrier_semaphore()
    for peer in peers:
        pl.semaphore_signal(barrier, inc=1, device_id=peer, device_id_type=MESH)
    pl.semaphore_wait(barrier, len(peers))


def all_peers(tensor_size):
    part, replica, tensor = where_am_i()
    total = 2 * tensor_size
    me = replica * tensor_size + tensor
    found = []
    for step in range(1, total):
        other = lax.rem(me + step, total)
        found.append((other, (part, other // tensor_size, lax.rem(other, tensor_size))))
    return me, found


def tensor_peers(tensor_size):
    part, replica, tensor = where_am_i()
    found = []
    for step in range(1, tensor_size):
        other = lax.rem(tensor + step, tensor_size)
        found.append((other, (part, replica, other)))
    return tensor, found


def remote(src, dst, send, recv, peer):
    return pltpu.make_async_remote_copy(
        src_ref=src, dst_ref=dst, send_sem=send, recv_sem=recv, device_id=peer, device_id_type=MESH
    )


def head_kernel(
    size, rank, x_ref, id_ref, a_hbm, wq_hbm, wkv_hbm, bq_hbm, bkv_hbm, out_ref, ids_ref,
    a_all, wq, wkv, bq, bkv, folded, g_ref, feat_in, features, shrink,
    red_x, red_land, red_mine, red_all, spread, out_x, out_in,
    load_a, load, send_id, recv_id, send_ft, recv_ft, send_up, recv_up, send_dn, recv_dn,
    send_y, recv_y, send_a, recv_a, send_b, recv_b, send_o, recv_o,
):
    part, replica, tensor = where_am_i()
    loads = [
        pltpu.make_async_copy(src, dst, load.at[at])
        for at, (src, dst) in enumerate(
            ((wq_hbm, wq), (wkv_hbm, wkv), (bq_hbm, bq), (bkv_hbm, bkv))
        )
    ]
    pair = 6 * rank
    pairs = a_all.shape[0] // pair

    def load_pair(at):
        spot = pl.ds(pl.multiple_of(at * pair, pair), pair)
        return pltpu.make_async_copy(a_hbm.at[spot], a_all.at[spot], load_a.at[at])

    for at in range(pairs):
        load_pair(at).start()
    for copy in loads:
        copy.start()
    rows, model = x_ref.shape
    batch = rows * size
    every = 2 * batch
    part_cols = model // size
    half = part_cols // 2
    for at in range(size):
        lo = x_ref[:, at * part_cols : at * part_cols + half]
        hi = x_ref[:, at * part_cols + half : (at + 1) * part_cols]
        folded[at] = jnp.concatenate([lo, hi], 0).astype(jnp.bfloat16)
    me, everyone = all_peers(size)
    _, peers = tensor_peers(size)
    greet([peer for _, peer in everyone])
    copies = []
    for step, (other, peer) in enumerate(everyone):
        copy = remote(
            folded.at[lax.rem(other, size)], feat_in.at[me], send_ft.at[step], recv_ft.at[step], peer
        )
        copy.start()
        copies.append(copy)
        copy = remote(id_ref, ids_ref.at[me], send_id.at[step], recv_id.at[step], peer)
        copy.start()
        copies.append(copy)
    feat_in[me] = folded[tensor]
    ids_ref[me] = id_ref[...]
    depth = size // 2
    level, side = tensor // 2, lax.rem(tensor, 2)
    above = (part, replica, lax.rem(tensor + 2, size))
    below = (part, replica, lax.rem(tensor + size - 2, size))
    across = (part, replica, level * 2 + 1 - side)

    def block(at):
        return jnp.clip(at, 0, depth - 1) * 2 + side

    def up(step):
        at = block(level - step)
        return remote(g_ref.at[at], g_ref.at[at], send_up.at[step], recv_up.at[step], above)

    def up_in(step):
        at = block(level - step - 1)
        return remote(g_ref.at[at], g_ref.at[at], send_up.at[step], recv_up.at[step], above)

    def down(step):
        at = block(level + step)
        return remote(g_ref.at[at], g_ref.at[at], send_dn.at[step], recv_dn.at[step], below)

    def down_in(step):
        at = block(level + step + 1)
        return remote(g_ref.at[at], g_ref.at[at], send_dn.at[step], recv_dn.at[step], below)

    def cross(at_level):
        at = jnp.clip(at_level, 0, depth - 1)
        return remote(
            g_ref.at[at * 2 + side], g_ref.at[at * 2 + side], send_y.at[at], recv_y.at[at], across
        )

    def cross_in(at):
        return remote(
            g_ref.at[at * 2 + 1 - side], g_ref.at[at * 2 + 1 - side], send_y.at[at], recv_y.at[at], across
        )

    g_ref[tensor] = folded[...]
    has_above, has_below = level < depth - 1, level > 0

    @pl.when(has_above)
    def _():
        up(0).start()

    @pl.when(has_below)
    def _():
        down(0).start()

    cross(level).start()
    slots = bq.shape[0] // rank

    def shrink_step(at, carry):
        load_pair(at).wait()
        spot = pl.ds(pl.multiple_of(at * pair, pair), pair)
        product = lax.dot_general(
            features[...], a_all[spot, :], (((1,), (1,)), ((), ())),
            preferred_element_type=jnp.float32,
        )
        local = ids_ref[...].reshape(every, 128)[:, :1] - replica * slots
        first = lax.broadcasted_iota(jnp.int32, product.shape, 1) + (2 * at - local) * (3 * rank)
        shrink[...] += jnp.where(
            jnp.logical_and(first >= 0, first < 3 * rank), product, 0.0
        )
        return carry

    for step in range(depth - 1):

        @pl.when(level - step - 1 >= 0)
        def _():
            up_in(step).wait_recv()
            if step + 1 < depth - 1:

                @pl.when(has_above)
                def _():
                    up(step + 1).start()

            cross(level - step - 1).start()

        @pl.when(level + step + 1 < depth)
        def _():
            down_in(step).wait_recv()
            if step + 1 < depth - 1:

                @pl.when(has_below)
                def _():
                    down(step + 1).start()

            cross(level + step + 1).start()

        if step == 0:
            for copy in copies:
                copy.wait()
            taken = feat_in[...].astype(jnp.float32)
            features[:, :half] = taken[:, :rows].reshape(every, half).astype(jnp.bfloat16)
            features[:, half:] = taken[:, rows:].reshape(every, half).astype(jnp.bfloat16)
            shrink[...] = jnp.zeros_like(shrink)
        lax.fori_loop(
            step * pairs // (depth - 1), (step + 1) * pairs // (depth - 1), shrink_step, 0
        )

    total = shrink[...]
    third = 3 * rank
    total = total[:, :third] + total[:, third:]
    total = jnp.concatenate([total, jnp.zeros((every, red_x.shape[2] - third), jnp.float32)], 1)
    red_x[...] = total.reshape(red_x.shape)
    sent = []
    for step, (other, peer) in enumerate(peers):
        copy = remote(red_x.at[other], red_land.at[tensor], send_a.at[step], recv_a.at[step], peer)
        copy.start()
        sent.append(copy)
    red_land[tensor] = red_x[tensor]
    for copy in sent:
        copy.wait()
    total = red_land[0]
    for step in range(1, size):
        total = total + red_land[step]
    red_mine[...] = total.astype(jnp.bfloat16)
    sent = []
    for step, (other, peer) in enumerate(peers):
        copy = remote(red_mine, red_all.at[tensor], send_b.at[step], recv_b.at[step], peer)
        copy.start()
        sent.append(copy)
    red_all[tensor] = red_mine[...]

    for at in range(depth):
        cross_in(at).wait_recv()
    loads[0].wait()
    loads[1].wait()
    qcols, kvcols = wq.shape[1], wkv.shape[0]

    def base_step(at, carry):
        base_q, base_kv = carry
        taken = g_ref[:, at].astype(jnp.float32)
        for side_at in range(2):
            left = taken[:, side_at * rows : (side_at + 1) * rows].reshape(batch, half)
            left = left.astype(jnp.bfloat16)
            spot = pl.ds(pl.multiple_of(at * part_cols + side_at * half, half), half)
            base_q = base_q + jnp.dot(left, wq[spot, :], preferred_element_type=jnp.float32)
            base_kv = base_kv + lax.dot_general(
                left, wkv[:, spot], (((1,), (1,)), ((), ())), preferred_element_type=jnp.float32
            )
        return base_q, base_kv

    base_q, base_kv = lax.fori_loop(
        0, size, base_step,
        (jnp.zeros((batch, qcols), jnp.float32), jnp.zeros((batch, kvcols), jnp.float32)),
    )
    for copy in sent:
        copy.wait()
    shrunk = red_all[...].reshape(every, red_all.shape[2])
    local_id = ids_ref[...].reshape(every, 128)[:, :1] - replica * slots
    wide = 512
    for at in range(0, bq.shape[0], wide):
        place = lax.broadcasted_iota(jnp.int32, (rank, wide), 1) + at
        place = place - lax.broadcasted_iota(jnp.int32, (rank, wide), 0) * slots
        expand = jnp.where(jnp.logical_and(place >= 0, place < slots), 1.0, 0.0).astype(jnp.bfloat16)
        piece = jnp.dot(shrunk[:, :rank], expand, preferred_element_type=jnp.float32)
        slot = lax.rem(lax.broadcasted_iota(jnp.int32, piece.shape, 1), slots)
        spread[:, at : at + wide] = jnp.where(slot == local_id, piece, 0.0).astype(jnp.bfloat16)
    for copy in loads[2:]:
        copy.wait()
    delta_q = jnp.dot(spread[...], bq[...], preferred_element_type=jnp.float32)
    wider = shrunk.astype(jnp.float32)
    shrunk_kv = jnp.where(
        tensor < size // 2, wider[:, rank : 2 * rank], wider[:, 2 * rank : 3 * rank]
    ).astype(jnp.bfloat16)
    delta_kv = jnp.zeros((every, kvcols), jnp.float32)
    for at in range(0, bkv.shape[0], wide):
        product = lax.dot_general(
            shrunk_kv, bkv[at : at + wide, :], (((1,), (1,)), ((), ())),
            preferred_element_type=jnp.float32,
        )
        first = lax.broadcasted_iota(jnp.int32, product.shape, 1) + at - local_id * kvcols
        product = jnp.where(jnp.logical_and(first >= 0, first < kvcols), product, 0.0)
        lanes = product[:, :128]
        for lane in range(128, wide, 128):
            lanes = lanes + product[:, lane : lane + 128]
        for lane in range(0, 128, kvcols):
            delta_kv = delta_kv + lanes[:, lane : lane + kvcols]
    rest = out_x.shape[2] - qcols - kvcols
    out_x[...] = jnp.concatenate(
        [delta_q, delta_kv, jnp.zeros((every, rest), jnp.float32)], 1
    ).reshape(out_x.shape)
    own = pl.ds(replica * size, size)
    out_x[own] = out_x[own] + jnp.concatenate(
        [base_q, base_kv, jnp.zeros((batch, rest), jnp.float32)], 1
    ).reshape(size, rows, out_x.shape[2])
    sent = []
    for step, (other, peer) in enumerate(everyone):
        copy = remote(out_x.at[other], out_in.at[me], send_o.at[step], recv_o.at[step], peer)
        copy.start()
        sent.append(copy)
    out_in[me] = out_x[me]
    for step in range(depth - 1):

        @pl.when(jnp.logical_and(has_above, level - step >= 0))
        def _():
            up(step).wait_send()

        @pl.when(jnp.logical_and(has_below, level + step < depth))
        def _():
            down(step).wait_send()

    for at in range(depth):
        cross(at).wait_send()
    for copy in sent:
        copy.wait()
    out_ref[...] = out_in[:size] + out_in[size:]


def tail_kernel(
    size, chunks, rank, ids_ref, x_ref, ao_hbm, wo_hbm, bo_hbm, out_ref,
    ao, wo, bo, heads_in, red_x, red_land, red_mine, red_all, spread,
    near, away, land_y, land_z, d_out, d_in,
    load, send_h, recv_h, send_a, recv_a, send_b, recv_b, send_d, recv_d,
    send_y, recv_y, send_z, recv_z,
):
    part, replica, tensor = where_am_i()
    loads = [
        pltpu.make_async_copy(src, dst, load.at[at])
        for at, (src, dst) in enumerate(((ao_hbm, ao), (wo_hbm, wo), (bo_hbm, bo)))
    ]
    for copy in loads:
        copy.start()
    me, everyone = all_peers(size)
    _, peers = tensor_peers(size)
    greet([peer for _, peer in everyone])
    depth = size // 2
    level, side = tensor // 2, lax.rem(tensor, 2)
    across = (part, replica, level * 2 + 1 - side)
    rows = heads_in.shape[1]
    batch = rows * size
    every = 2 * batch
    model = out_ref.shape[1]
    half = model // 2
    slots = bo.shape[0] // rank

    sent = []
    for step, (other, peer) in enumerate(everyone):
        copy = remote(
            x_ref.at[lax.rem(other, size)], heads_in.at[me], send_h.at[step], recv_h.at[step], peer
        )
        copy.start()
        sent.append(copy)
    heads_in[me] = x_ref[tensor]
    for copy in sent:
        copy.wait()
    heads = heads_in[...].reshape(every, heads_in.shape[2]).astype(jnp.bfloat16)
    local_id = ids_ref[:, :1] - replica * slots
    loads[0].wait()
    wide = 512
    total = None
    for at in range(0, ao.shape[0], wide):
        product = lax.dot_general(
            heads, ao[at : at + wide, :], (((1,), (1,)), ((), ())), preferred_element_type=jnp.float32
        )
        first = lax.broadcasted_iota(jnp.int32, product.shape, 1) + at - local_id * rank
        product = jnp.where(jnp.logical_and(first >= 0, first < rank), product, 0.0)
        for lane in range(0, wide, 128):
            piece = product[:, lane : lane + 128]
            total = piece if total is None else total + piece
    if rank == 64:
        total = total + pltpu.roll(total, 64, 1)
    red_x[...] = total.reshape(red_x.shape)
    sent = []
    for step, (other, peer) in enumerate(peers):
        copy = remote(red_x.at[other], red_land.at[tensor], send_a.at[step], recv_a.at[step], peer)
        copy.start()
        sent.append(copy)
    red_land[tensor] = red_x[tensor]

    own = heads_in[pl.ds(replica * size, size)].reshape(batch, heads_in.shape[2]).astype(jnp.bfloat16)
    loads[1].wait()
    width = half // chunks
    y_copies = []
    for chunk in range(chunks):
        parts = []
        for start in (chunk * width, half + chunk * width):
            term = jnp.dot(own, wo[:, start : start + width], preferred_element_type=jnp.float32)
            parts.append(term.reshape(size, rows, width))
        term = jnp.concatenate(parts, 1).reshape(depth, 2, 2 * rows, width)
        here = jnp.where(side == 0, term[:, 0], term[:, 1])
        there = jnp.where(side == 0, term[:, 1], term[:, 0])
        away[chunk] = there.astype(jnp.bfloat16)
        copy = remote(away.at[chunk], land_y.at[chunk], send_y.at[chunk], recv_y.at[chunk], across)
        copy.start()
        y_copies.append(copy)
        near[chunk] = here

    for copy in sent:
        copy.wait()
    total = red_land[0]
    for step in range(1, size):
        total = total + red_land[step]
    red_mine[...] = total.astype(jnp.bfloat16)
    sent = []
    for step, (other, peer) in enumerate(peers):
        copy = remote(red_mine, red_all.at[tensor], send_b.at[step], recv_b.at[step], peer)
        copy.start()
        sent.append(copy)
    red_all[tensor] = red_mine[...]

    z_copies = []

    def pass_on(chunk):
        y_copies[chunk].wait()
        near[chunk] = near[chunk] + land_y[chunk].astype(jnp.float32)
        away[chunk] = near[chunk].astype(jnp.bfloat16)
        for step in range(1, depth):
            other = lax.rem(level + step, depth)
            copy = remote(
                away.at[chunk, other], land_z.at[chunk, level],
                send_z.at[chunk, step - 1], recv_z.at[chunk, step - 1],
                (part, replica, other * 2 + side),
            )
            copy.start()
            z_copies.append(copy)
        land_z[chunk, level] = away[chunk, level]

    early = min(1, chunks)
    for chunk in range(early):
        pass_on(chunk)
    for copy in sent:
        copy.wait()
    shrunk = red_all[...].reshape(every, red_all.shape[2])
    for at in range(0, bo.shape[0], wide):
        shape = (shrunk.shape[1], wide)
        place = lax.broadcasted_iota(jnp.int32, shape, 1) + at
        place = place - lax.broadcasted_iota(jnp.int32, shape, 0) * slots
        expand = jnp.where(jnp.logical_and(place >= 0, place < slots), 1.0, 0.0).astype(jnp.bfloat16)
        piece = jnp.dot(shrunk, expand, preferred_element_type=jnp.float32)
        slot = lax.rem(lax.broadcasted_iota(jnp.int32, piece.shape, 1), slots)
        spread[:, at : at + wide] = jnp.where(slot == local_id, piece, 0.0).astype(jnp.bfloat16)
    loads[2].wait()
    cols = bo.shape[1]
    delta = jnp.concatenate(
        [
            jnp.dot(
                spread[...], bo[:, at : at + cols // 2], preferred_element_type=jnp.float32
            ).reshape(2 * size, rows, cols // 2)
            for at in (0, cols // 2)
        ],
        1,
    )
    d_out[...] = delta.astype(jnp.bfloat16)
    d_copies = []
    for step, (other, peer) in enumerate(everyone):
        copy = remote(d_out.at[other], d_in.at[me], send_d.at[step], recv_d.at[step], peer)
        copy.start()
        d_copies.append(copy)
    d_in[me] = d_out[me]
    for chunk in range(early, chunks):
        pass_on(chunk)
    count = depth - 1
    for chunk in range(chunks):
        for copy in z_copies[chunk * count : (chunk + 1) * count]:
            copy.wait()
        total = land_z[chunk, 0].astype(jnp.float32)
        for at in range(1, depth):
            total = total + land_z[chunk, at].astype(jnp.float32)
        out_ref[:, chunk * width : (chunk + 1) * width] = total[:rows]
        out_ref[:, half + chunk * width : half + (chunk + 1) * width] = total[rows:]
    for copy in d_copies:
        copy.wait()
    for at in range(size):
        extra = d_in[at].astype(jnp.float32) + d_in[size + at].astype(jnp.float32)
        start = at * cols
        out_ref[:, start : start + cols // 2] += extra[:rows]
        out_ref[:, start + cols // 2 : start + cols] += extra[rows:]


def shards(
    hidden,
    gain,
    request_adapter_index,
    lengths,
    rotated_key_cache,
    earlier_value_cache,
    query_weight,
    key_value_weight,
    output_weight,
    down_weight_qkv,
    up_weight_query,
    up_weight_key_value,
    down_weight_output,
    up_weight_output,
):
    size = lax.axis_size("tensor")
    own_rows, model_width = hidden.shape
    batch_rows = own_rows * size
    every_row = 2 * batch_rows
    hidden_wide = hidden.astype(jnp.float32)
    mean_square = jnp.mean(hidden_wide * hidden_wide, axis=-1, keepdims=True)
    normalized_input = hidden_wide * lax.rsqrt(mean_square + EPSILON) * gain
    id_tile = jnp.broadcast_to(request_adapter_index[:, None], (own_rows, 128))
    depth = size // 2
    dma = pltpu.SemaphoreType.DMA
    steps = max(depth - 1, 1)
    vmem, f32, bf16 = pltpu.VMEM, jnp.float32, jnp.bfloat16
    double = 2 * own_rows
    part_cols, slots, triple = down_weight_qkv.shape
    rank_size = up_weight_query.shape[0]
    query_cols = query_weight.shape[1]
    kv_cols = key_value_weight.shape[1]
    padded = -(-(query_cols + kv_cols) // 128) * 128
    red = -(-triple // 128) * 128
    down_qkv = down_weight_qkv.transpose(1, 2, 0).reshape(slots * triple, part_cols)
    up_q = up_weight_query.reshape(rank_size * slots, query_cols)
    up_kv = up_weight_key_value.transpose(1, 2, 0).reshape(slots * kv_cols, rank_size)
    kv_weight = key_value_weight.T
    half = part_cols // 2
    arrived, id_tiles = pl.pallas_call(
        functools.partial(head_kernel, size, rank_size),
        out_shape=(
            jax.ShapeDtypeStruct((size, own_rows, padded), f32),
            jax.ShapeDtypeStruct((2 * size, own_rows, 128), jnp.int32),
        ),
        in_specs=[pl.BlockSpec(memory_space=vmem)] * 2 + [pl.BlockSpec(memory_space=pl.ANY)] * 5,
        out_specs=(pl.BlockSpec(memory_space=vmem), pl.BlockSpec(memory_space=vmem)),
        scratch_shapes=[
            vmem(down_qkv.shape, bf16),
            vmem(query_weight.shape, bf16),
            vmem(kv_weight.shape, bf16),
            vmem(up_q.shape, bf16),
            vmem(up_kv.shape, bf16),
            vmem((size, double, half), bf16),
            vmem((size, size, double, half), bf16),
            vmem((2 * size, double, half), bf16),
            vmem((every_row, part_cols), bf16),
            vmem((every_row, 2 * triple), f32),
            vmem((size, double, red), f32),
            vmem((size, double, red), f32),
            vmem((double, red), bf16),
            vmem((size, double, red), bf16),
            vmem((every_row, rank_size * slots), bf16),
            vmem((2 * size, own_rows, padded), f32),
            vmem((2 * size, own_rows, padded), f32),
            dma((slots // 2,)),
            dma((4,)),
        ]
        + [dma((2 * size - 1,))] * 4
        + [dma((steps,))] * 4
        + [dma((depth,))] * 2
        + [dma((size - 1,))] * 4
        + [dma((2 * size - 1,))] * 2,
        compiler_params=pltpu.CompilerParams(
            collective_id=0, has_side_effects=True, vmem_limit_bytes=VMEM_LIMIT
        ),
    )(normalized_input, id_tile, down_qkv, query_weight, kv_weight, up_q, up_kv)
    arrived = arrived.astype(bf16).transpose(1, 0, 2)
    query_rows = arrived[:, :, :query_cols].reshape(own_rows, size * query_cols)
    kv_rows = arrived[:, :, query_cols : query_cols + kv_cols].reshape(own_rows, size * kv_cols)
    head_count = query_rows.shape[1] // HEAD_WIDTH
    kv_heads = kv_rows.shape[1] // (2 * HEAD_WIDTH)
    q_rot = rotate(
        query_rows.reshape(own_rows, head_count, HEAD_WIDTH).astype(jnp.float32), lengths
    ).astype(jnp.bfloat16)
    q_rot = q_rot.reshape(own_rows, kv_heads, head_count // kv_heads, HEAD_WIDTH)
    k_rot = rotate(
        kv_rows[:, : kv_heads * HEAD_WIDTH]
        .reshape(own_rows, kv_heads, HEAD_WIDTH)
        .astype(jnp.float32),
        lengths,
    ).astype(jnp.bfloat16)
    fresh_values = kv_rows[:, kv_heads * HEAD_WIDTH :].reshape(own_rows, kv_heads, HEAD_WIDTH)
    mixed = attend(q_rot, k_rot, fresh_values, rotated_key_cache, earlier_value_cache, lengths)
    head_cols = mixed.shape[1] // size
    leaving = mixed.astype(jnp.float32).reshape(own_rows, size, head_cols).transpose(1, 0, 2)
    rank_out, _, out_cols = up_weight_output.shape
    down_table = down_weight_output.transpose(1, 2, 0).reshape(-1, head_cols)
    up_table = up_weight_output.reshape(rank_out * slots, out_cols)
    chunks = 4
    width = model_width // 2 // chunks
    double = 2 * own_rows
    vmem, f32, bf16 = pltpu.VMEM, jnp.float32, jnp.bfloat16
    out = pl.pallas_call(
        functools.partial(tail_kernel, size, chunks, rank_out),
        out_shape=jax.ShapeDtypeStruct((own_rows, model_width), f32),
        in_specs=[pl.BlockSpec(memory_space=vmem)] * 2 + [pl.BlockSpec(memory_space=pl.ANY)] * 3,
        out_specs=pl.BlockSpec(memory_space=vmem),
        scratch_shapes=[
            vmem(down_table.shape, bf16),
            vmem(output_weight.shape, bf16),
            vmem(up_table.shape, bf16),
            vmem((2 * size, own_rows, head_cols), f32),
            vmem((size, double, 128), f32),
            vmem((size, double, 128), f32),
            vmem((double, 128), bf16),
            vmem((size, double, 128), bf16),
            vmem((every_row, rank_out * slots), bf16),
            vmem((chunks, depth, double, width), f32),
            vmem((chunks, depth, double, width), bf16),
            vmem((chunks, depth, double, width), bf16),
            vmem((chunks, depth, double, width), bf16),
            vmem((2 * size, double, out_cols // 2), bf16),
            vmem((2 * size, double, out_cols // 2), bf16),
            dma((3,)),
            dma((2 * size - 1,)),
            dma((2 * size - 1,)),
            dma((size - 1,)),
            dma((size - 1,)),
            dma((size - 1,)),
            dma((size - 1,)),
            dma((2 * size - 1,)),
            dma((2 * size - 1,)),
            dma((chunks,)),
            dma((chunks,)),
            dma((chunks, steps)),
            dma((chunks, steps)),
        ],
        compiler_params=pltpu.CompilerParams(
            collective_id=3, has_side_effects=True, vmem_limit_bytes=VMEM_LIMIT
        ),
    )(id_tiles.reshape(every_row, 128), leaving, down_table, output_weight, up_table)
    return out.astype(jnp.bfloat16)


def solution(mesh):
    return jax.shard_map(
        shards,
        mesh=mesh,
        in_specs=(
            P(("parts", "replica", "tensor"), None),
            P(),
            P(("parts", "replica", "tensor")),
            P(("parts", "replica", "tensor")),
            P(("parts", "replica", "tensor"), None, None, None),
            P(("parts", "replica", "tensor"), None, None, None),
            P(None, "tensor"),
            P(None, "tensor"),
            P("tensor", None),
            P("tensor", "replica", None),
            P(None, "replica", "tensor"),
            P(None, "replica", "tensor"),
            P("tensor", "replica", None),
            P(None, "replica", "tensor"),
        ),
        out_specs=P(("parts", "replica", "tensor"), None),
        check_vma=False,
    )
```

```python
import functools

import jax
import jax.numpy as jnp
from jax import lax
from jax.experimental import pallas as pl
from jax.experimental.pallas import tpu as pltpu
from jax.sharding import PartitionSpec as P

HEAD_WIDTH = 128
EPSILON = 1e-05
MESH = pl.DeviceIdType.MESH
VMEM_LIMIT = 48 * 1024 * 1024


def rotate(heads_in, positions):
    half_dim = HEAD_WIDTH // 2
    frequency = 10000.0 ** (-jnp.arange(half_dim, dtype=jnp.float32) * 2.0 / HEAD_WIDTH)
    angles = positions.astype(jnp.float32)[:, None] * frequency[None, :]
    cosine = jnp.cos(angles)[:, None, :]
    sine_part = jnp.sin(angles)[:, None, :]
    first_half = heads_in[..., :half_dim]
    second_half = heads_in[..., half_dim:]
    return jnp.concatenate(
        [
            first_half * cosine - second_half * sine_part,
            second_half * cosine + first_half * sine_part,
        ],
        -1,
    )


def attend(q_rot, k_rot, fresh_values, rotated_key_cache, earlier_value_cache, lengths):
    score_scale = HEAD_WIDTH ** (-0.5)
    scores = (
        jnp.einsum("rgjd,rgld->rgjl", q_rot, rotated_key_cache, preferred_element_type=jnp.float32)
        * score_scale
    )
    cached = rotated_key_cache.shape[2]
    visible = (jnp.arange(cached, dtype=jnp.int32)[None, :] < lengths[:, None])[:, None, None, :]
    scores = jnp.where(visible, scores, -jnp.inf)
    score_new = (
        jnp.einsum("rgjd,rgd->rgj", q_rot, k_rot, preferred_element_type=jnp.float32) * score_scale
    )
    highest = jnp.maximum(jnp.max(scores, axis=-1), score_new)
    weights_cache = jnp.exp(scores - highest[..., None])
    weight_new = jnp.exp(score_new - highest)
    denominator = jnp.sum(weights_cache, axis=-1) + weight_new
    weights_cache = (weights_cache / denominator[..., None]).astype(jnp.bfloat16)
    weight_new = (weight_new / denominator).astype(jnp.bfloat16)
    mixed = jnp.einsum(
        "rgjl,rgld->rgjd", weights_cache, earlier_value_cache, preferred_element_type=jnp.float32
    )
    mixed = (
        mixed
        + weight_new.astype(jnp.float32)[..., None]
        * fresh_values.astype(jnp.float32)[:, :, None, :]
    )
    return mixed.astype(jnp.bfloat16).reshape(q_rot.shape[0], -1)


def where_am_i():
    return lax.axis_index("parts"), lax.axis_index("replica"), lax.axis_index("tensor")


def greet(peers):
    barrier = pltpu.get_barrier_semaphore()
    for peer in peers:
        pl.semaphore_signal(barrier, inc=1, device_id=peer, device_id_type=MESH)
    pl.semaphore_wait(barrier, len(peers))


def all_peers(tensor_size):
    part, replica, tensor = where_am_i()
    total = 2 * tensor_size
    me = replica * tensor_size + tensor
    found = []
    for step in range(1, total):
        other = lax.rem(me + step, total)
        found.append((other, (part, other // tensor_size, lax.rem(other, tensor_size))))
    return me, found


def tensor_peers(tensor_size):
    part, replica, tensor = where_am_i()
    found = []
    for step in range(1, tensor_size):
        other = lax.rem(tensor + step, tensor_size)
        found.append((other, (part, replica, other)))
    return tensor, found


def remote(src, dst, send, recv, peer):
    return pltpu.make_async_remote_copy(
        src_ref=src, dst_ref=dst, send_sem=send, recv_sem=recv, device_id=peer, device_id_type=MESH
    )


def head_kernel(
    size, rank, x_ref, id_ref, a_hbm, wq_hbm, wkv_hbm, bq_hbm, bkv_hbm, out_ref, ids_ref,
    a_all, wq, wkv, bq, bkv, folded, g_ref, feat_in, features, shrink,
    red_x, red_land, red_mine, red_all, spread, out_x, out_in,
    load_a, load, send_id, recv_id, send_ft, recv_ft, send_up, recv_up, send_dn, recv_dn,
    send_y, recv_y, send_a, recv_a, send_b, recv_b, send_o, recv_o,
):
    part, replica, tensor = where_am_i()
    loads = [
        pltpu.make_async_copy(src, dst, load.at[at])
        for at, (src, dst) in enumerate(
            ((wq_hbm, wq), (wkv_hbm, wkv), (bq_hbm, bq), (bkv_hbm, bkv))
        )
    ]
    pair = 6 * rank
    pairs = a_all.shape[0] // pair

    def load_pair(at):
        spot = pl.ds(pl.multiple_of(at * pair, pair), pair)
        return pltpu.make_async_copy(a_hbm.at[spot], a_all.at[spot], load_a.at[at])

    for at in range(pairs):
        load_pair(at).start()
    for copy in loads:
        copy.start()
    rows, model = x_ref.shape
    batch = rows * size
    every = 2 * batch
    part_cols = model // size
    half = part_cols // 2
    for at in range(size):
        lo = x_ref[:, at * part_cols : at * part_cols + half]
        hi = x_ref[:, at * part_cols + half : (at + 1) * part_cols]
        folded[at] = jnp.concatenate([lo, hi], 0).astype(jnp.bfloat16)
    me, everyone = all_peers(size)
    _, peers = tensor_peers(size)
    greet([peer for _, peer in everyone])
    copies = []
    for step, (other, peer) in enumerate(everyone):
        copy = remote(
            folded.at[lax.rem(other, size)], feat_in.at[me], send_ft.at[step], recv_ft.at[step], peer
        )
        copy.start()
        copies.append(copy)
        copy = remote(id_ref, ids_ref.at[me], send_id.at[step], recv_id.at[step], peer)
        copy.start()
        copies.append(copy)
    feat_in[me] = folded[tensor]
    ids_ref[me] = id_ref[...]
    depth = size // 2
    level, side = tensor // 2, lax.rem(tensor, 2)
    above = (part, replica, lax.rem(tensor + 2, size))
    below = (part, replica, lax.rem(tensor + size - 2, size))
    across = (part, replica, level * 2 + 1 - side)

    def block(at):
        return jnp.clip(at, 0, depth - 1) * 2 + side

    def up(step):
        at = block(level - step)
        return remote(g_ref.at[at], g_ref.at[at], send_up.at[step], recv_up.at[step], above)

    def up_in(step):
        at = block(level - step - 1)
        return remote(g_ref.at[at], g_ref.at[at], send_up.at[step], recv_up.at[step], above)

    def down(step):
        at = block(level + step)
        return remote(g_ref.at[at], g_ref.at[at], send_dn.at[step], recv_dn.at[step], below)

    def down_in(step):
        at = block(level + step + 1)
        return remote(g_ref.at[at], g_ref.at[at], send_dn.at[step], recv_dn.at[step], below)

    def cross(at_level):
        at = jnp.clip(at_level, 0, depth - 1)
        return remote(
            g_ref.at[at * 2 + side], g_ref.at[at * 2 + side], send_y.at[at], recv_y.at[at], across
        )

    def cross_in(at):
        return remote(
            g_ref.at[at * 2 + 1 - side], g_ref.at[at * 2 + 1 - side], send_y.at[at], recv_y.at[at], across
        )

    g_ref[tensor] = folded[...]
    has_above, has_below = level < depth - 1, level > 0

    @pl.when(has_above)
    def _():
        up(0).start()

    @pl.when(has_below)
    def _():
        down(0).start()

    cross(level).start()
    slots = bq.shape[0] // rank

    def shrink_step(at, carry):
        load_pair(at).wait()
        spot = pl.ds(pl.multiple_of(at * pair, pair), pair)
        product = lax.dot_general(
            features[...], a_all[spot, :], (((1,), (1,)), ((), ())),
            preferred_element_type=jnp.float32,
        )
        local = ids_ref[...].reshape(every, 128)[:, :1] - replica * slots
        first = lax.broadcasted_iota(jnp.int32, product.shape, 1) + (2 * at - local) * (3 * rank)
        shrink[...] += jnp.where(
            jnp.logical_and(first >= 0, first < 3 * rank), product, 0.0
        )
        return carry

    for step in range(depth - 1):

        @pl.when(level - step - 1 >= 0)
        def _():
            up_in(step).wait_recv()
            if step + 1 < depth - 1:

                @pl.when(has_above)
                def _():
                    up(step + 1).start()

            cross(level - step - 1).start()

        @pl.when(level + step + 1 < depth)
        def _():
            down_in(step).wait_recv()
            if step + 1 < depth - 1:

                @pl.when(has_below)
                def _():
                    down(step + 1).start()

            cross(level + step + 1).start()

        if step == 0:
            for copy in copies:
                copy.wait()
            taken = feat_in[...].astype(jnp.float32)
            features[:, :half] = taken[:, :rows].reshape(every, half).astype(jnp.bfloat16)
            features[:, half:] = taken[:, rows:].reshape(every, half).astype(jnp.bfloat16)
            shrink[...] = jnp.zeros_like(shrink)
        lax.fori_loop(
            step * pairs // (depth - 1), (step + 1) * pairs // (depth - 1), shrink_step, 0
        )

    total = shrink[...]
    third = 3 * rank
    total = total[:, :third] + total[:, third:]
    total = jnp.concatenate([total, jnp.zeros((every, red_x.shape[2] - third), jnp.float32)], 1)
    red_x[...] = total.reshape(red_x.shape)
    sent = []
    for step, (other, peer) in enumerate(peers):
        copy = remote(red_x.at[other], red_land.at[tensor], send_a.at[step], recv_a.at[step], peer)
        copy.start()
        sent.append(copy)
    red_land[tensor] = red_x[tensor]
    for copy in sent:
        copy.wait()
    total = red_land[0]
    for step in range(1, size):
        total = total + red_land[step]
    red_mine[...] = total.astype(jnp.bfloat16)
    sent = []
    for step, (other, peer) in enumerate(peers):
        copy = remote(red_mine, red_all.at[tensor], send_b.at[step], recv_b.at[step], peer)
        copy.start()
        sent.append(copy)
    red_all[tensor] = red_mine[...]

    for at in range(depth):
        cross_in(at).wait_recv()
    loads[0].wait()
    loads[1].wait()
    qcols, kvcols = wq.shape[1], wkv.shape[0]

    def base_step(at, carry):
        base_q, base_kv = carry
        taken = g_ref[:, at].astype(jnp.float32)
        for side_at in range(2):
            left = taken[:, side_at * rows : (side_at + 1) * rows].reshape(batch, half)
            left = left.astype(jnp.bfloat16)
            spot = pl.ds(pl.multiple_of(at * part_cols + side_at * half, half), half)
            base_q = base_q + jnp.dot(left, wq[spot, :], preferred_element_type=jnp.float32)
            base_kv = base_kv + lax.dot_general(
                left, wkv[:, spot], (((1,), (1,)), ((), ())), preferred_element_type=jnp.float32
            )
        return base_q, base_kv

    base_q, base_kv = lax.fori_loop(
        0, size, base_step,
        (jnp.zeros((batch, qcols), jnp.float32), jnp.zeros((batch, kvcols), jnp.float32)),
    )
    for copy in sent:
        copy.wait()
    shrunk = red_all[...].reshape(every, red_all.shape[2])
    local_id = ids_ref[...].reshape(every, 128)[:, :1] - replica * slots
    wide = 512
    for at in range(0, bq.shape[0], wide):
        place = lax.broadcasted_iota(jnp.int32, (rank, wide), 1) + at
        place = place - lax.broadcasted_iota(jnp.int32, (rank, wide), 0) * slots
        expand = jnp.where(jnp.logical_and(place >= 0, place < slots), 1.0, 0.0).astype(jnp.bfloat16)
        piece = jnp.dot(shrunk[:, :rank], expand, preferred_element_type=jnp.float32)
        slot = lax.rem(lax.broadcasted_iota(jnp.int32, piece.shape, 1), slots)
        spread[:, at : at + wide] = jnp.where(slot == local_id, piece, 0.0).astype(jnp.bfloat16)
    for copy in loads[2:]:
        copy.wait()
    delta_q = jnp.dot(spread[...], bq[...], preferred_element_type=jnp.float32)
    wider = shrunk.astype(jnp.float32)
    shrunk_kv = jnp.where(
        tensor < size // 2, wider[:, rank : 2 * rank], wider[:, 2 * rank : 3 * rank]
    ).astype(jnp.bfloat16)
    delta_kv = jnp.zeros((every, kvcols), jnp.float32)
    for at in range(0, bkv.shape[0], wide):
        product = lax.dot_general(
            shrunk_kv, bkv[at : at + wide, :], (((1,), (1,)), ((), ())),
            preferred_element_type=jnp.float32,
        )
        first = lax.broadcasted_iota(jnp.int32, product.shape, 1) + at - local_id * kvcols
        product = jnp.where(jnp.logical_and(first >= 0, first < kvcols), product, 0.0)
        lanes = product[:, :128]
        for lane in range(128, wide, 128):
            lanes = lanes + product[:, lane : lane + 128]
        for lane in range(0, 128, kvcols):
            delta_kv = delta_kv + lanes[:, lane : lane + kvcols]
    rest = out_x.shape[2] - qcols - kvcols
    out_x[...] = jnp.concatenate(
        [delta_q, delta_kv, jnp.zeros((every, rest), jnp.float32)], 1
    ).reshape(out_x.shape)
    own = pl.ds(replica * size, size)
    out_x[own] = out_x[own] + jnp.concatenate(
        [base_q, base_kv, jnp.zeros((batch, rest), jnp.float32)], 1
    ).reshape(size, rows, out_x.shape[2])
    sent = []
    for step, (other, peer) in enumerate(everyone):
        copy = remote(out_x.at[other], out_in.at[me], send_o.at[step], recv_o.at[step], peer)
        copy.start()
        sent.append(copy)
    out_in[me] = out_x[me]
    for step in range(depth - 1):

        @pl.when(jnp.logical_and(has_above, level - step >= 0))
        def _():
            up(step).wait_send()

        @pl.when(jnp.logical_and(has_below, level + step < depth))
        def _():
            down(step).wait_send()

    for at in range(depth):
        cross(at).wait_send()
    for copy in sent:
        copy.wait()
    out_ref[...] = out_in[:size] + out_in[size:]


def tail_kernel(
    size, chunks, rank, ids_ref, x_ref, ao_hbm, wo_hbm, bo_hbm, out_ref,
    ao, wo, bo, heads_in, red_x, red_land, red_mine, red_all, spread,
    near, away, land_y, land_z, d_out, d_in,
    load, send_h, recv_h, send_a, recv_a, send_b, recv_b, send_d, recv_d,
    send_y, recv_y, send_z, recv_z,
):
    part, replica, tensor = where_am_i()
    loads = [
        pltpu.make_async_copy(src, dst, load.at[at])
        for at, (src, dst) in enumerate(((ao_hbm, ao), (wo_hbm, wo), (bo_hbm, bo)))
    ]
    for copy in loads:
        copy.start()
    me, everyone = all_peers(size)
    _, peers = tensor_peers(size)
    greet([peer for _, peer in everyone])
    depth = size // 2
    level, side = tensor // 2, lax.rem(tensor, 2)
    across = (part, replica, level * 2 + 1 - side)
    rows = heads_in.shape[1]
    batch = rows * size
    every = 2 * batch
    model = out_ref.shape[1]
    half = model // 2
    slots = bo.shape[0] // rank

    sent = []
    for step, (other, peer) in enumerate(everyone):
        copy = remote(
            x_ref.at[lax.rem(other, size)], heads_in.at[me], send_h.at[step], recv_h.at[step], peer
        )
        copy.start()
        sent.append(copy)
    heads_in[me] = x_ref[tensor]
    for copy in sent:
        copy.wait()
    heads = heads_in[...].reshape(every, heads_in.shape[2]).astype(jnp.bfloat16)
    local_id = ids_ref[:, :1] - replica * slots
    loads[0].wait()
    wide = 512
    total = None
    for at in range(0, ao.shape[0], wide):
        product = lax.dot_general(
            heads, ao[at : at + wide, :], (((1,), (1,)), ((), ())), preferred_element_type=jnp.float32
        )
        first = lax.broadcasted_iota(jnp.int32, product.shape, 1) + at - local_id * rank
        product = jnp.where(jnp.logical_and(first >= 0, first < rank), product, 0.0)
        for lane in range(0, wide, 128):
            piece = product[:, lane : lane + 128]
            total = piece if total is None else total + piece
    if rank == 64:
        total = total + pltpu.roll(total, 64, 1)
    red_x[...] = total.reshape(red_x.shape)
    sent = []
    for step, (other, peer) in enumerate(peers):
        copy = remote(red_x.at[other], red_land.at[tensor], send_a.at[step], recv_a.at[step], peer)
        copy.start()
        sent.append(copy)
    red_land[tensor] = red_x[tensor]

    own = heads_in[pl.ds(replica * size, size)].reshape(batch, heads_in.shape[2]).astype(jnp.bfloat16)
    loads[1].wait()
    width = half // chunks
    y_copies = []
    for chunk in range(chunks):
        parts = []
        for start in (chunk * width, half + chunk * width):
            term = jnp.dot(own, wo[:, start : start + width], preferred_element_type=jnp.float32)
            parts.append(term.reshape(size, rows, width))
        term = jnp.concatenate(parts, 1).reshape(depth, 2, 2 * rows, width)
        here = jnp.where(side == 0, term[:, 0], term[:, 1])
        there = jnp.where(side == 0, term[:, 1], term[:, 0])
        away[chunk] = there.astype(jnp.bfloat16)
        copy = remote(away.at[chunk], land_y.at[chunk], send_y.at[chunk], recv_y.at[chunk], across)
        copy.start()
        y_copies.append(copy)
        near[chunk] = here

    for copy in sent:
        copy.wait()
    total = red_land[0]
    for step in range(1, size):
        total = total + red_land[step]
    red_mine[...] = total.astype(jnp.bfloat16)
    sent = []
    for step, (other, peer) in enumerate(peers):
        copy = remote(red_mine, red_all.at[tensor], send_b.at[step], recv_b.at[step], peer)
        copy.start()
        sent.append(copy)
    red_all[tensor] = red_mine[...]

    z_copies = []

    def pass_on(chunk):
        y_copies[chunk].wait()
        near[chunk] = near[chunk] + land_y[chunk].astype(jnp.float32)
        away[chunk] = near[chunk].astype(jnp.bfloat16)
        for step in range(1, depth):
            other = lax.rem(level + step, depth)
            copy = remote(
                away.at[chunk, other], land_z.at[chunk, level],
                send_z.at[chunk, step - 1], recv_z.at[chunk, step - 1],
                (part, replica, other * 2 + side),
            )
            copy.start()
            z_copies.append(copy)
        land_z[chunk, level] = away[chunk, level]

    early = min(1, chunks)
    for chunk in range(early):
        pass_on(chunk)
    for copy in sent:
        copy.wait()
    shrunk = red_all[...].reshape(every, red_all.shape[2])
    for at in range(0, bo.shape[0], wide):
        shape = (shrunk.shape[1], wide)
        place = lax.broadcasted_iota(jnp.int32, shape, 1) + at
        place = place - lax.broadcasted_iota(jnp.int32, shape, 0) * slots
        expand = jnp.where(jnp.logical_and(place >= 0, place < slots), 1.0, 0.0).astype(jnp.bfloat16)
        piece = jnp.dot(shrunk, expand, preferred_element_type=jnp.float32)
        slot = lax.rem(lax.broadcasted_iota(jnp.int32, piece.shape, 1), slots)
        spread[:, at : at + wide] = jnp.where(slot == local_id, piece, 0.0).astype(jnp.bfloat16)
    loads[2].wait()
    cols = bo.shape[1]
    delta = jnp.concatenate(
        [
            jnp.dot(
                spread[...], bo[:, at : at + cols // 2], preferred_element_type=jnp.float32
            ).reshape(2 * size, rows, cols // 2)
            for at in (0, cols // 2)
        ],
        1,
    )
    d_out[...] = delta.astype(jnp.bfloat16)
    d_copies = []
    for step, (other, peer) in enumerate(everyone):
        copy = remote(d_out.at[other], d_in.at[me], send_d.at[step], recv_d.at[step], peer)
        copy.start()
        d_copies.append(copy)
    d_in[me] = d_out[me]
    for chunk in range(early, chunks):
        pass_on(chunk)
    count = depth - 1
    for chunk in range(chunks):
        for copy in z_copies[chunk * count : (chunk + 1) * count]:
            copy.wait()
        total = land_z[chunk, 0].astype(jnp.float32)
        for at in range(1, depth):
            total = total + land_z[chunk, at].astype(jnp.float32)
        out_ref[:, chunk * width : (chunk + 1) * width] = total[:rows]
        out_ref[:, half + chunk * width : half + (chunk + 1) * width] = total[rows:]
    for copy in d_copies:
        copy.wait()
    for at in range(size):
        extra = d_in[at].astype(jnp.float32) + d_in[size + at].astype(jnp.float32)
        start = at * cols
        out_ref[:, start : start + cols // 2] += extra[:rows]
        out_ref[:, start + cols // 2 : start + cols] += extra[rows:]


def shards(
    hidden,
    gain,
    request_adapter_index,
    lengths,
    rotated_key_cache,
    earlier_value_cache,
    query_weight,
    key_value_weight,
    output_weight,
    down_weight_qkv,
    up_weight_query,
    up_weight_key_value,
    down_weight_output,
    up_weight_output,
):
    size = lax.axis_size("tensor")
    own_rows, model_width = hidden.shape
    batch_rows = own_rows * size
    every_row = 2 * batch_rows
    hidden_wide = hidden.astype(jnp.float32)
    mean_square = jnp.mean(hidden_wide * hidden_wide, axis=-1, keepdims=True)
    normalized_input = hidden_wide * lax.rsqrt(mean_square + EPSILON) * gain
    id_tile = jnp.broadcast_to(request_adapter_index[:, None], (own_rows, 128))
    depth = size // 2
    dma = pltpu.SemaphoreType.DMA
    steps = max(depth - 1, 1)
    vmem, f32, bf16 = pltpu.VMEM, jnp.float32, jnp.bfloat16
    double = 2 * own_rows
    part_cols, slots, triple = down_weight_qkv.shape
    rank_size = up_weight_query.shape[0]
    query_cols = query_weight.shape[1]
    kv_cols = key_value_weight.shape[1]
    padded = -(-(query_cols + kv_cols) // 128) * 128
    red = -(-triple // 128) * 128
    down_qkv = down_weight_qkv.transpose(1, 2, 0).reshape(slots * triple, part_cols)
    up_q = up_weight_query.reshape(rank_size * slots, query_cols)
    up_kv = up_weight_key_value.transpose(1, 2, 0).reshape(slots * kv_cols, rank_size)
    kv_weight = key_value_weight.T
    half = part_cols // 2
    arrived, id_tiles = pl.pallas_call(
        functools.partial(head_kernel, size, rank_size),
        out_shape=(
            jax.ShapeDtypeStruct((size, own_rows, padded), f32),
            jax.ShapeDtypeStruct((2 * size, own_rows, 128), jnp.int32),
        ),
        in_specs=[pl.BlockSpec(memory_space=vmem)] * 2 + [pl.BlockSpec(memory_space=pl.ANY)] * 5,
        out_specs=(pl.BlockSpec(memory_space=vmem), pl.BlockSpec(memory_space=vmem)),
        scratch_shapes=[
            vmem(down_qkv.shape, bf16),
            vmem(query_weight.shape, bf16),
            vmem(kv_weight.shape, bf16),
            vmem(up_q.shape, bf16),
            vmem(up_kv.shape, bf16),
            vmem((size, double, half), bf16),
            vmem((size, size, double, half), bf16),
            vmem((2 * size, double, half), bf16),
            vmem((every_row, part_cols), bf16),
            vmem((every_row, 2 * triple), f32),
            vmem((size, double, red), f32),
            vmem((size, double, red), f32),
            vmem((double, red), bf16),
            vmem((size, double, red), bf16),
            vmem((every_row, rank_size * slots), bf16),
            vmem((2 * size, own_rows, padded), f32),
            vmem((2 * size, own_rows, padded), f32),
            dma((slots // 2,)),
            dma((4,)),
        ]
        + [dma((2 * size - 1,))] * 4
        + [dma((steps,))] * 4
        + [dma((depth,))] * 2
        + [dma((size - 1,))] * 4
        + [dma((2 * size - 1,))] * 2,
        compiler_params=pltpu.CompilerParams(
            collective_id=0, has_side_effects=True, vmem_limit_bytes=VMEM_LIMIT
        ),
    )(normalized_input, id_tile, down_qkv, query_weight, kv_weight, up_q, up_kv)
    arrived = arrived.astype(bf16).transpose(1, 0, 2)
    query_rows = arrived[:, :, :query_cols].reshape(own_rows, size * query_cols)
    kv_rows = arrived[:, :, query_cols : query_cols + kv_cols].reshape(own_rows, size * kv_cols)
    head_count = query_rows.shape[1] // HEAD_WIDTH
    kv_heads = kv_rows.shape[1] // (2 * HEAD_WIDTH)
    q_rot = rotate(
        query_rows.reshape(own_rows, head_count, HEAD_WIDTH).astype(jnp.float32), lengths
    ).astype(jnp.bfloat16)
    q_rot = q_rot.reshape(own_rows, kv_heads, head_count // kv_heads, HEAD_WIDTH)
    k_rot = rotate(
        kv_rows[:, : kv_heads * HEAD_WIDTH]
        .reshape(own_rows, kv_heads, HEAD_WIDTH)
        .astype(jnp.float32),
        lengths,
    ).astype(jnp.bfloat16)
    fresh_values = kv_rows[:, kv_heads * HEAD_WIDTH :].reshape(own_rows, kv_heads, HEAD_WIDTH)
    mixed = attend(q_rot, k_rot, fresh_values, rotated_key_cache, earlier_value_cache, lengths)
    head_cols = mixed.shape[1] // size
    leaving = mixed.astype(jnp.float32).reshape(own_rows, size, head_cols).transpose(1, 0, 2)
    rank_out, _, out_cols = up_weight_output.shape
    down_table = down_weight_output.transpose(1, 2, 0).reshape(-1, head_cols)
    up_table = up_weight_output.reshape(rank_out * slots, out_cols)
    chunks = 2
    width = model_width // 2 // chunks
    double = 2 * own_rows
    vmem, f32, bf16 = pltpu.VMEM, jnp.float32, jnp.bfloat16
    out = pl.pallas_call(
        functools.partial(tail_kernel, size, chunks, rank_out),
        out_shape=jax.ShapeDtypeStruct((own_rows, model_width), f32),
        in_specs=[pl.BlockSpec(memory_space=vmem)] * 2 + [pl.BlockSpec(memory_space=pl.ANY)] * 3,
        out_specs=pl.BlockSpec(memory_space=vmem),
        scratch_shapes=[
            vmem(down_table.shape, bf16),
            vmem(output_weight.shape, bf16),
            vmem(up_table.shape, bf16),
            vmem((2 * size, own_rows, head_cols), f32),
            vmem((size, double, 128), f32),
            vmem((size, double, 128), f32),
            vmem((double, 128), bf16),
            vmem((size, double, 128), bf16),
            vmem((every_row, rank_out * slots), bf16),
            vmem((chunks, depth, double, width), f32),
            vmem((chunks, depth, double, width), bf16),
            vmem((chunks, depth, double, width), bf16),
            vmem((chunks, depth, double, width), bf16),
            vmem((2 * size, double, out_cols // 2), bf16),
            vmem((2 * size, double, out_cols // 2), bf16),
            dma((3,)),
            dma((2 * size - 1,)),
            dma((2 * size - 1,)),
            dma((size - 1,)),
            dma((size - 1,)),
            dma((size - 1,)),
            dma((size - 1,)),
            dma((2 * size - 1,)),
            dma((2 * size - 1,)),
            dma((chunks,)),
            dma((chunks,)),
            dma((chunks, steps)),
            dma((chunks, steps)),
        ],
        compiler_params=pltpu.CompilerParams(
            collective_id=3, has_side_effects=True, vmem_limit_bytes=VMEM_LIMIT
        ),
    )(id_tiles.reshape(every_row, 128), leaving, down_table, output_weight, up_table)
    return out.astype(jnp.bfloat16)


def solution(mesh):
    return jax.shard_map(
        shards,
        mesh=mesh,
        in_specs=(
            P(("parts", "replica", "tensor"), None),
            P(),
            P(("parts", "replica", "tensor")),
            P(("parts", "replica", "tensor")),
            P(("parts", "replica", "tensor"), None, None, None),
            P(("parts", "replica", "tensor"), None, None, None),
            P(None, "tensor"),
            P(None, "tensor"),
            P("tensor", None),
            P("tensor", "replica", None),
            P(None, "replica", "tensor"),
            P(None, "replica", "tensor"),
            P("tensor", "replica", None),
            P(None, "replica", "tensor"),
        ),
        out_specs=P(("parts", "replica", "tensor"), None),
        check_vma=False,
    )
```
